32 devices in a mesh: dp: 4 (over y, x), fsdp: 8 (over z, core).
Axes of the slice: x: 2, y: 2, z: 4, core: 2. Of those that a mesh axis runs over, the one named last changes fastest.
Arguments:
- grads: bfloat16 [4, 32, 512, 4096], P('dp', None, None, 'fsdp'), may hold values from -5 to 5
- left_stats: float32 [32, 8, 512, 512], P('fsdp', 'dp'), as said below
- right_stats: float32 [32, 8, 512, 512], P('fsdp', 'dp'), as said below
- left_root: float32 [32, 8, 512, 512], P('fsdp', 'dp'), as said below
- right_root: float32 [32, 8, 512, 512], P('fsdp', 'dp'), as said below
Outputs:
- update: bfloat16 [32, 512, 4096], P(None, None, 'fsdp')
The draws below stay inside these ranges and needn't reach their ends.
Inputs may be any that keep to these rules, and one draw needn't show every extreme that they name: `left_stats`: symmetric. `right_stats`: symmetric. `left_root`: symmetric. `right_root`: symmetric.
All inputs are finite; a program needn't handle non-finite values.
Results may differ from the reference program's by a relative error of at most 0.012.
Values may be sent and summed in bfloat16 or wider, within the bound.
No kernel may reach another device: no remote copies, remote signals or barrier semaphores. Data moves between devices by JAX's collectives and lax.ppermute only.
A program may use at most 256 MiB of HBM per device.

```python
import math
import jax
import jax.numpy as jnp
from jax import lax

BLK = 512
COLS = 4096
SLABS = 32
BCOLS = 8
N_DP = 4


def symmetric_blocks(key, diag_low, diag_high, spread):
    first, second = jax.random.split(key)
    noise = jax.random.uniform(first, (SLABS, BCOLS, BLK, BLK), jnp.float32, -spread, spread)
    noise = 0.5 * (noise + jnp.swapaxes(noise, -1, -2))
    diagonal = jax.random.uniform(second, (SLABS, BCOLS, BLK), jnp.float32, diag_low, diag_high)
    identity = jnp.eye(BLK, dtype=jnp.float32)
    return noise * (1.0 - identity) + identity * diagonal[..., None]


def draw_left_stats(key, part):
    key = jax.random.fold_in(key, 11)
    return symmetric_blocks(key, 0.8, 1.3, 0.6 / math.sqrt(BLK))


def draw_right_stats(key, part):
    key = jax.random.fold_in(key, 12)
    return symmetric_blocks(key, 0.8, 1.3, 0.6 / math.sqrt(BLK))


def draw_left_root(key, part):
    key = jax.random.fold_in(key, 13)
    return symmetric_blocks(key, 0.8, 1.1, 0.4 / math.sqrt(BLK))


def draw_right_root(key, part):
    key = jax.random.fold_in(key, 14)
    return symmetric_blocks(key, 0.8, 1.1, 0.4 / math.sqrt(BLK))


def level_of(stream_key, shape, shards, smallest, largest):
    def one(position, blocks):
        draws = jax.random.uniform(jax.random.fold_in(jax.random.fold_in(stream_key, 6), position), (blocks,), jnp.float32, smallest / len(shards), largest / len(shards))
        return jnp.repeat(jnp.exp(draws), shape[position] // blocks).reshape((-1,) + (1,) * (len(shape) - position - 1))

    gain = one(*shards[0])
    for cut in shards[1:]:
        gain = gain * one(*cut)
    return gain


def bell_draw(key, shape, scale, most, shards=(), held_as=jnp.bfloat16):
    entries = jax.random.normal(key, shape, jnp.float32) * scale
    if len(shards) > 0:
        entries = level_of(key, shape, shards, -0.22, 0.18) * entries
    return jnp.clip(entries, min=-most, max=most).astype(held_as)


def setup_inputs(seed: int = 0) -> dict:
    seeds = jax.random.split(jax.random.key(seed), 6)
    grads = bell_draw(seeds[0], (N_DP, SLABS, BLK, COLS), 0.35, 5.0, ((0, 4), (3, 8)))
    left_stats = draw_left_stats(jax.random.fold_in(seeds[5], 71), 0)
    right_stats = draw_right_stats(jax.random.fold_in(seeds[5], 71), 0)
    left_root = draw_left_root(jax.random.fold_in(seeds[5], 71), 0)
    right_root = draw_right_root(jax.random.fold_in(seeds[5], 71), 0)
    return dict(grads=grads, left_stats=left_stats, right_stats=right_stats, left_root=left_root, right_root=right_root)


EXACT = lax.Precision.HIGHEST
ema_decay = 0.999


def refine(root, stats):
    square = jnp.einsum("bij,bjk->bik", root, root, precision=EXACT)
    fourth = jnp.einsum("bij,bjk->bik", square, square, precision=EXACT)
    coupled = jnp.einsum("bij,bjk->bik", fourth, stats, precision=EXACT)
    identity = jnp.eye(root.shape[-1], dtype=jnp.float32)
    factor = (5.0 * identity - coupled) * 0.25
    return jnp.einsum("bij,bjk->bik", root, factor, precision=EXACT)


def precondition(items):
    block_grads, left_stats, right_stats, left_root, right_root = items
    wide = block_grads.astype(jnp.float32)
    left = ema_decay * left_stats + (1.0 - ema_decay) * jnp.einsum("bik,bjk->bij", wide, wide, precision=EXACT)
    right = ema_decay * right_stats + (1.0 - ema_decay) * jnp.einsum("bki,bkj->bij", wide, wide, precision=EXACT)
    new_left = refine(left_root, left)
    new_right = refine(right_root, right)
    halfway = jnp.einsum("bij,bjk->bik", new_left, wide, precision=EXACT)
    return jnp.einsum("bij,bjk->bik", halfway, new_right, precision=EXACT).astype(jnp.bfloat16)


def reference(grads, left_stats, right_stats, left_root, right_root):
    total = jnp.zeros(grads.shape[1:], jnp.float32)
    for replica in range(N_DP):
        total = total + grads[replica].astype(jnp.float32)
    summed = total.astype(jnp.bfloat16)
    blocks = summed.reshape(SLABS, BLK, BCOLS, BLK).transpose(0, 2, 1, 3)
    result = lax.map(precondition, (blocks, left_stats, right_stats, left_root, right_root))
    return result.transpose(0, 2, 1, 3).reshape(SLABS, BLK, COLS)
```

```python
import functools

import jax
import jax.numpy as jnp
from jax import lax
from jax.experimental import pallas as pl
from jax.experimental.pallas import tpu as pltpu
from jax.sharding import PartitionSpec as P

ema_decay = 0.999
MESH_AXES = ("dp", "fsdp")
VMEM_LIMIT = 60 * 1024 * 1024


def split(x):
    high = x.astype(jnp.bfloat16)
    low = (x - high.astype(jnp.float32)).astype(jnp.bfloat16)
    return high, low


def mm(a, b):
    return jnp.dot(a, b, preferred_element_type=jnp.float32)


def dot3(a, b):
    a_high, a_low = split(a)
    b_high, b_low = split(b)
    return mm(a_high, b_high) + (mm(a_high, b_low) + mm(a_low, b_high))


def fourth_kernel(left_ref, right_ref, left_out, right_out):
    for ref, out in ((left_ref, left_out), (right_ref, right_out)):
        root = ref[0, 0]
        square = dot3(root, root)
        out[0, 0] = dot3(square, square)


def fourth_powers(left_root, right_root):
    slabs, col_blocks, order, _ = left_root.shape
    spec = pl.BlockSpec((1, 1, order, order), lambda i, j: (i, j, 0, 0))
    shape = jax.ShapeDtypeStruct(left_root.shape, jnp.float32)
    count = slabs * col_blocks
    return pl.pallas_call(
        fourth_kernel,
        grid=(slabs, col_blocks),
        in_specs=[spec, spec],
        out_specs=[spec, spec],
        out_shape=[shape, shape],
        compiler_params=pltpu.CompilerParams(vmem_limit_bytes=VMEM_LIMIT),
        cost_estimate=pl.CostEstimate(
            flops=count * 4 * 3 * 2 * order**3, bytes_accessed=count * 16 * order**2, transcendentals=0
        ),
        name="fourth_powers",
    )(left_root, right_root)


def copy_all(copies):
    for copy in copies:
        copy.start()
    for copy in copies:
        copy.wait()


def pieces_of(ranks, inner):
    return [(d, k, e) for d in range(ranks) for k in range(ranks) for e in range(inner)]


def pack_kernel(ranks, inner, slot, per, inner_ref, grads_ref, out_ref, sems):
    rows = grads_ref.shape[1] // ranks
    mine = inner_ref[0]
    copies = []
    for at, (d, k, e) in enumerate(pieces_of(ranks, inner)):
        slab = ((d ^ k) * inner + (mine ^ e)) * per + slot
        copies.append(
            pltpu.make_async_copy(
                grads_ref.at[slab, pl.ds(d * rows, rows), :],
                out_ref.at[pl.ds(at * rows, rows), :],
                sems.at[at],
            )
        )
    copy_all(copies)


def pack(ranks, inner, slot, per, my_inner, grads):
    slabs, order, width = grads.shape
    count = ranks * ranks * inner
    return pl.pallas_call(
        functools.partial(pack_kernel, ranks, inner, slot, per),
        in_specs=[pl.BlockSpec(memory_space=pltpu.SMEM), pl.BlockSpec(memory_space=pl.ANY)],
        out_specs=pl.BlockSpec(memory_space=pl.ANY),
        out_shape=jax.ShapeDtypeStruct((slabs // per * order, width), grads.dtype),
        scratch_shapes=[pltpu.SemaphoreType.DMA((count,))],
        compiler_params=pltpu.CompilerParams(vmem_limit_bytes=VMEM_LIMIT),
        cost_estimate=pl.CostEstimate(
            flops=0, bytes_accessed=4 * slabs // per * order * width, transcendentals=0
        ),
        name="pack_slabs",
    )(my_inner, grads)


def unpack_kernel(ranks, inner, slot, per, inner_ref, got_ref, *rest):
    out_ref, sems = rest[-2], rest[-1]
    rows = out_ref.shape[1] // ranks
    mine = inner_ref[0]
    copies = []
    for at, (d, k, e) in enumerate(pieces_of(ranks, inner)):
        slab = ((d ^ k) * inner + (mine ^ e)) * per + slot
        copies.append(
            pltpu.make_async_copy(
                got_ref.at[pl.ds(at * rows, rows), :],
                out_ref.at[slab, pl.ds(d * rows, rows), :],
                sems.at[at],
            )
        )
    copy_all(copies)


def unpack(ranks, inner, slot, per, my_inner, got, shape, so_far):
    anywhere = pl.BlockSpec(memory_space=pl.ANY)
    operands = [my_inner, got] + ([] if so_far is None else [so_far])
    return pl.pallas_call(
        functools.partial(unpack_kernel, ranks, inner, slot, per),
        in_specs=[pl.BlockSpec(memory_space=pltpu.SMEM)] + [anywhere] * (len(operands) - 1),
        out_specs=anywhere,
        out_shape=jax.ShapeDtypeStruct(shape, got.dtype),
        scratch_shapes=[pltpu.SemaphoreType.DMA((ranks * ranks * inner,))],
        input_output_aliases={} if so_far is None else {2: 0},
        compiler_params=pltpu.CompilerParams(vmem_limit_bytes=VMEM_LIMIT),
        cost_estimate=pl.CostEstimate(flops=0, bytes_accessed=4 * got.size, transcendentals=0),
        name="unpack_slabs",
    )(*operands)


def refine(root, fourth, stats):
    order = root.shape[0]
    coupled = dot3(fourth, stats)
    on_diagonal = lax.broadcasted_iota(jnp.int32, (order, order), 0) == lax.broadcasted_iota(
        jnp.int32, (order, order), 1
    )
    factor = (jnp.where(on_diagonal, 5.0, 0.0) - coupled) * 0.25
    return dot3(root, factor)


def block_kernel(ranks, inner, steps, place_ref, *refs):
    count = ranks * inner
    pieces = refs[:count]
    left_stats, right_stats, left_root, right_root, left_fourth, right_fourth = refs[count : count + 6]
    outs = refs[count + 6 : 2 * count + 6]
    blocks, results = refs[2 * count + 6 :]
    rows, width = pieces[0].shape
    order = blocks.shape[1]
    outer_place, inner_place = place_ref[0], place_ref[1]
    step = pl.program_id(0)
    per_block = order // width

    def spot(k, e):
        shard = inner_place ^ e
        row = pl.multiple_of((outer_place ^ k) * rows, rows)
        column = pl.multiple_of((shard % per_block) * width, width)
        return shard // per_block, pl.ds(row, rows), pl.ds(column, width)

    @pl.when(step == 0)
    def _():
        for k in range(ranks):
            for e in range(inner):
                blocks[spot(k, e)] = pieces[k * inner + e][...]

    block = blocks[step]
    turned = block.T
    left = ema_decay * left_stats[0, 0] + (1.0 - ema_decay) * mm(block, turned)
    right = ema_decay * right_stats[0, 0] + (1.0 - ema_decay) * mm(turned, block)
    new_left = refine(left_root[0, 0], left_fourth[0, 0], left)
    new_right = refine(right_root[0, 0], right_fourth[0, 0], right)
    high, low = split(new_left)
    halfway = mm(high, block) + mm(low, block)
    results[step] = dot3(halfway, new_right).astype(results.dtype)

    @pl.when(step == steps - 1)
    def _():
        for k in range(ranks):
            for e in range(inner):
                outs[k * inner + e][...] = results[spot(k, e)]


def precondition(ranks, inner, slot, place, pieces, stats_and_roots):
    _, col_blocks, order, _ = stats_and_roots[0].shape
    rows, width = pieces[0].shape
    count = ranks * inner
    piece = pl.BlockSpec((rows, width), lambda j: (0, 0))
    matrix = pl.BlockSpec((1, 1, order, order), lambda j: (slot, j, 0, 0))
    return pl.pallas_call(
        functools.partial(block_kernel, ranks, inner, col_blocks),
        grid=(col_blocks,),
        in_specs=[pl.BlockSpec(memory_space=pltpu.SMEM)] + [piece] * count + [matrix] * 6,
        out_specs=[piece] * count,
        out_shape=[jax.ShapeDtypeStruct((rows, width), jnp.bfloat16)] * count,
        scratch_shapes=[pltpu.VMEM((col_blocks, order, order), jnp.bfloat16)] * 2,
        compiler_params=pltpu.CompilerParams(vmem_limit_bytes=VMEM_LIMIT),
        cost_estimate=pl.CostEstimate(
            flops=col_blocks * 19 * 2 * order**3,
            bytes_accessed=col_blocks * 28 * order**2,
            transcendentals=0,
        ),
        name="precondition",
    )(place, *pieces, *stats_and_roots)


def shards(ranks, fsdp, grads, left_stats, right_stats, left_root, right_root):
    per = left_stats.shape[0]
    inner = fsdp // ranks
    grads = grads[0]
    slabs, order, width = grads.shape
    rows = order // ranks
    f = lax.axis_index("fsdp")
    place = jnp.stack([f // inner, f % inner]).astype(jnp.int32)
    my_inner = place[1:]
    rounds = [(k, e) for k in range(ranks) for e in range(inner)]

    def number(d, a, b):
        return (d * ranks + a) * inner + b

    sources = [(d, a, b) for d in range(ranks) for a in range(ranks) for b in range(inner)]
    to_owner = {
        (k, e): [(number(d, a, b), number(a, d ^ k, b ^ e)) for d, a, b in sources] for k, e in rounds
    }
    to_column = {key: [(y, x) for x, y in pairs] for key, pairs in to_owner.items()}

    summed = []
    for slot in range(per):
        packed = pack(ranks, inner, slot, per, my_inner, grads)
        summed.append(lax.psum_scatter(packed, "dp", scatter_dimension=0, tiled=True))
    left_fourth, right_fourth = fourth_powers(left_root, right_root)
    summed[0], left_fourth, right_fourth = lax.optimization_barrier((summed[0], left_fourth, right_fourth))
    matrices = (left_stats, right_stats, left_root, right_root, left_fourth, right_fourth)
    out = None
    for slot in range(per):
        arrived = [
            lax.ppermute(summed[slot][at * rows : (at + 1) * rows], MESH_AXES, to_owner[key])
            for at, key in enumerate(rounds)
        ]
        done = precondition(ranks, inner, slot, place, arrived, matrices)
        back = [lax.ppermute(piece, MESH_AXES, to_column[key]) for piece, key in zip(done, rounds)]
        gathered = lax.all_gather(jnp.concatenate(back, axis=0), "dp", axis=0, tiled=True)
        out = unpack(ranks, inner, slot, per, my_inner, gathered, grads.shape, out)
    return out


def solution(mesh):
    placed = (
        P("dp", None, None, "fsdp"),
        P("fsdp", "dp", None, None),
        P("fsdp", "dp", None, None),
        P("fsdp", "dp", None, None),
        P("fsdp", "dp", None, None),
    )
    run = functools.partial(shards, mesh.shape["dp"], mesh.shape["fsdp"])
    return jax.shard_map(
        run, mesh=mesh, in_specs=placed, out_specs=P(None, None, "fsdp"), check_vma=False
    )
```

```python
import functools

import jax
import jax.numpy as jnp
from jax import lax
from jax.experimental import pallas as pl
from jax.experimental.pallas import tpu as pltpu
from jax.sharding import PartitionSpec as P

ema_decay = 0.999
MESH_AXES = ("dp", "fsdp")
VMEM_LIMIT = 60 * 1024 * 1024


def split(x):
    high = x.astype(jnp.bfloat16)
    low = (x - high.astype(jnp.float32)).astype(jnp.bfloat16)
    return high, low


def mm(a, b):
    return jnp.dot(a, b, preferred_element_type=jnp.float32)


def dot3(a, b):
    a_high, a_low = split(a)
    b_high, b_low = split(b)
    return mm(a_high, b_high) + (mm(a_high, b_low) + mm(a_low, b_high))


def fourth_kernel(left_ref, right_ref, left_out, right_out):
    for ref, out in ((left_ref, left_out), (right_ref, right_out)):
        root = ref[0, 0]
        square = dot3(root, root)
        out[0, 0] = dot3(square, square)


def fourth_powers(left_root, right_root):
    slabs, col_blocks, order, _ = left_root.shape
    spec = pl.BlockSpec((1, 1, order, order), lambda i, j: (i, j, 0, 0))
    shape = jax.ShapeDtypeStruct(left_root.shape, jnp.float32)
    count = slabs * col_blocks
    return pl.pallas_call(
        fourth_kernel,
        grid=(slabs, col_blocks),
        in_specs=[spec, spec],
        out_specs=[spec, spec],
        out_shape=[shape, shape],
        compiler_params=pltpu.CompilerParams(vmem_limit_bytes=VMEM_LIMIT),
        cost_estimate=pl.CostEstimate(
            flops=count * 4 * 3 * 2 * order**3, bytes_accessed=count * 16 * order**2, transcendentals=0
        ),
        name="fourth_powers",
    )(left_root, right_root)


def slab_of(k, e, outer_place, inner_place, inner):
    return (outer_place ^ k) * inner + (inner_place ^ e)


def pack_kernel(ranks, inner, place_ref, grads_ref, out_ref):
    rows = grads_ref.shape[2]
    d = pl.program_id(0)
    for k in range(ranks):
        for e in range(inner):
            at = (k * inner + e) * rows
            out_ref[at : at + rows] = grads_ref[slab_of(k, e, d, place_ref[1], inner), 0]


def pack(ranks, inner, slot, per, place, grads):
    slabs, order, width = grads.shape
    owners, rows = slabs // per, order // ranks
    return pl.pallas_call(
        functools.partial(pack_kernel, ranks, inner),
        grid=(ranks,),
        in_specs=[
            pl.BlockSpec(memory_space=pltpu.SMEM),
            pl.BlockSpec((owners, 1, rows, width), lambda d: (0, slot, d, 0)),
        ],
        out_specs=pl.BlockSpec((owners * rows, width), lambda d: (d, 0)),
        out_shape=jax.ShapeDtypeStruct((owners * order, width), grads.dtype),
        compiler_params=pltpu.CompilerParams(vmem_limit_bytes=VMEM_LIMIT),
        cost_estimate=pl.CostEstimate(
            flops=0, bytes_accessed=4 * owners * order * width, transcendentals=0
        ),
        name="pack_slabs",
    )(place, grads.reshape(owners, per, order, width))


def unpack_kernel(ranks, inner, place_ref, got_ref, *rest):
    out_ref = rest[-1]
    rows = out_ref.shape[2]
    for k in range(ranks):
        for e in range(inner):
            at = (k * inner + e) * rows
            out_ref[slab_of(k, e, place_ref[0], place_ref[1], inner), 0] = got_ref[at : at + rows]


def unpack(ranks, inner, slot, per, place, got, so_far):
    order = got.shape[0] // (ranks * inner)
    width, owners, rows = got.shape[1], ranks * inner, order // ranks
    operands = [place, got] + ([] if so_far is None else [so_far])
    return pl.pallas_call(
        functools.partial(unpack_kernel, ranks, inner),
        grid=(ranks,),
        in_specs=[
            pl.BlockSpec(memory_space=pltpu.SMEM),
            pl.BlockSpec((owners * rows, width), lambda d: (d, 0)),
        ]
        + [pl.BlockSpec(memory_space=pl.ANY)] * (len(operands) - 2),
        out_specs=pl.BlockSpec((owners, 1, rows, width), lambda d: (0, slot, d, 0)),
        out_shape=jax.ShapeDtypeStruct((owners, per, order, width), got.dtype),
        input_output_aliases={} if so_far is None else {2: 0},
        compiler_params=pltpu.CompilerParams(vmem_limit_bytes=VMEM_LIMIT),
        cost_estimate=pl.CostEstimate(flops=0, bytes_accessed=4 * got.size, transcendentals=0),
        name="unpack_slabs",
    )(*operands)


def route_kernel(ranks, inner, place_ref, *refs):
    taken, outs, held = refs[:ranks], refs[ranks:-1], refs[-1]
    rows = outs[0].shape[0]
    turn, inner_place = place_ref[2] ^ place_ref[0], place_ref[1]
    for k in range(ranks):
        held[k] = taken[k][...]
    for m in range(ranks):
        for e in range(inner):
            start = pl.multiple_of((inner_place ^ e) * rows, rows)
            outs[m * inner + e][...] = held[turn ^ m, pl.ds(start, rows), :]


def route(ranks, inner, place, taken):
    rows, width = taken[0].shape[0] // inner, taken[0].shape[1]
    vmem = pl.BlockSpec(memory_space=pltpu.VMEM)
    return pl.pallas_call(
        functools.partial(route_kernel, ranks, inner),
        in_specs=[pl.BlockSpec(memory_space=pltpu.SMEM)] + [vmem] * ranks,
        out_specs=[vmem] * (ranks * inner),
        out_shape=[jax.ShapeDtypeStruct((rows, width), taken[0].dtype)] * (ranks * inner),
        scratch_shapes=[pltpu.VMEM((ranks, inner * rows, width), taken[0].dtype)],
        compiler_params=pltpu.CompilerParams(vmem_limit_bytes=VMEM_LIMIT // 4),
        cost_estimate=pl.CostEstimate(
            flops=0, bytes_accessed=4 * ranks * taken[0].size, transcendentals=0
        ),
        name="route",
    )(place, *taken)


def refine(root, fourth, stats):
    order = root.shape[0]
    coupled = dot3(fourth, stats)
    on_diagonal = lax.broadcasted_iota(jnp.int32, (order, order), 0) == lax.broadcasted_iota(
        jnp.int32, (order, order), 1
    )
    factor = (jnp.where(on_diagonal, 5.0, 0.0) - coupled) * 0.25
    return dot3(root, factor)


def block_kernel(ranks, inner, steps, place_ref, *refs):
    count = ranks * inner
    pieces = refs[:count]
    left_stats, right_stats, left_root, right_root, left_fourth, right_fourth = refs[count : count + 6]
    outs = refs[count + 6 : count + 6 + ranks]
    blocks, results = refs[count + 6 + ranks :]
    rows, width = pieces[0].shape
    order = blocks.shape[1]
    outer_place, inner_place = place_ref[0], place_ref[1]
    step = pl.program_id(0)
    per_block = order // width

    def spot(rank, shard):
        row = pl.multiple_of(rank * rows, rows)
        column = pl.multiple_of((shard % per_block) * width, width)
        return shard // per_block, pl.ds(row, rows), pl.ds(column, width)

    @pl.when(step == 0)
    def _():
        for k in range(ranks):
            for e in range(inner):
                blocks[spot(outer_place ^ k, inner_place ^ e)] = pieces[k * inner + e][...]

    block = blocks[step]
    turned = block.T
    left = ema_decay * left_stats[0, 0] + (1.0 - ema_decay) * mm(block, turned)
    right = ema_decay * right_stats[0, 0] + (1.0 - ema_decay) * mm(turned, block)
    new_left = refine(left_root[0, 0], left_fourth[0, 0], left)
    new_right = refine(right_root[0, 0], right_fourth[0, 0], right)
    high, low = split(new_left)
    halfway = mm(high, block) + mm(low, block)
    results[step] = dot3(halfway, new_right).astype(results.dtype)

    @pl.when(step == steps - 1)
    def _():
        for k in range(ranks):
            for b in range(inner):
                outs[k][b * rows : (b + 1) * rows] = results[spot(place_ref[2] ^ k, b)]


def precondition(ranks, inner, slot, place, pieces, stats_and_roots):
    _, col_blocks, order, _ = stats_and_roots[0].shape
    rows, width = pieces[0].shape
    count = ranks * inner
    piece = pl.BlockSpec((rows, width), lambda j: (0, 0))
    strip = pl.BlockSpec((inner * rows, width), lambda j: (0, 0))
    matrix = pl.BlockSpec((1, 1, order, order), lambda j: (slot, j, 0, 0))
    return pl.pallas_call(
        functools.partial(block_kernel, ranks, inner, col_blocks),
        grid=(col_blocks,),
        in_specs=[pl.BlockSpec(memory_space=pltpu.SMEM)] + [piece] * count + [matrix] * 6,
        out_specs=[strip] * ranks,
        out_shape=[jax.ShapeDtypeStruct((inner * rows, width), jnp.bfloat16)] * ranks,
        scratch_shapes=[pltpu.VMEM((col_blocks, order, order), jnp.bfloat16)] * 2,
        compiler_params=pltpu.CompilerParams(vmem_limit_bytes=VMEM_LIMIT),
        cost_estimate=pl.CostEstimate(
            flops=col_blocks * 19 * 2 * order**3,
            bytes_accessed=col_blocks * 28 * order**2,
            transcendentals=0,
        ),
        name="precondition",
    )(place, *pieces, *stats_and_roots)


def shards(ranks, fsdp, grads, left_stats, right_stats, left_root, right_root):
    per = left_stats.shape[0]
    inner = fsdp // ranks
    grads = grads[0]
    slabs, order, width = grads.shape
    rows = order // ranks
    f = lax.axis_index("fsdp")
    place = jnp.stack([f // inner, f % inner, lax.axis_index("dp")]).astype(jnp.int32)
    rounds = [(k, e) for k in range(ranks) for e in range(inner)]

    def number(d, a, b):
        return (d * ranks + a) * inner + b

    sources = [(d, a, b) for d in range(ranks) for a in range(ranks) for b in range(inner)]
    to_owner = {
        (k, e): [(number(d, a, b), number(a, d ^ k, b ^ e)) for d, a, b in sources] for k, e in rounds
    }
    to_row = [[(d, d ^ k) for d in range(ranks)] for k in range(ranks)]
    to_column = {
        (m, e): [(a * inner + b, (a ^ m) * inner + (b ^ e)) for a in range(ranks) for b in range(inner)]
        for m, e in rounds
    }

    summed = []
    for slot in range(per):
        packed = pack(ranks, inner, slot, per, place, grads)
        summed.append(lax.psum_scatter(packed, "dp", scatter_dimension=0, tiled=True))
    left_fourth, right_fourth = fourth_powers(left_root, right_root)
    summed[0], left_fourth, right_fourth = lax.optimization_barrier((summed[0], left_fourth, right_fourth))
    matrices = (left_stats, right_stats, left_root, right_root, left_fourth, right_fourth)
    out = None
    for slot in range(per):
        arrived = [
            lax.ppermute(summed[slot][at * rows : (at + 1) * rows], MESH_AXES, to_owner[key])
            for at, key in enumerate(rounds)
        ]
        strips = precondition(ranks, inner, slot, place, arrived, matrices)
        strips = [strips[0]] + [lax.ppermute(strips[k], "dp", to_row[k]) for k in range(1, ranks)]
        routed = route(ranks, inner, place, strips)
        back = [routed[0]] + [
            lax.ppermute(piece, "fsdp", to_column[key]) for piece, key in zip(routed[1:], rounds[1:])
        ]
        gathered = lax.all_gather(jnp.concatenate(back, axis=0), "dp", axis=0, tiled=True)
        out = unpack(ranks, inner, slot, per, place, gathered, out)
    return out.reshape(grads.shape)


def solution(mesh):
    placed = (
        P("dp", None, None, "fsdp"),
        P("fsdp", "dp", None, None),
        P("fsdp", "dp", None, None),
        P("fsdp", "dp", None, None),
        P("fsdp", "dp", None, None),
    )
    run = functools.partial(shards, mesh.shape["dp"], mesh.shape["fsdp"])
    return jax.shard_map(
        run, mesh=mesh, in_specs=placed, out_specs=P(None, None, "fsdp"), check_vma=False
    )
```

```python
import functools

import jax
import jax.numpy as jnp
from jax import lax
from jax.experimental import pallas as pl
from jax.experimental.pallas import tpu as pltpu
from jax.sharding import PartitionSpec as P

ema_decay = 0.999
MESH_AXES = ("dp", "fsdp")
VMEM_LIMIT = 60 * 1024 * 1024


def split(x):
    high = x.astype(jnp.bfloat16)
    low = (x - high.astype(jnp.float32)).astype(jnp.bfloat16)
    return high, low


def mm(a, b):
    return jnp.dot(a, b, preferred_element_type=jnp.float32)


def dot3(a, b):
    a_high, a_low = split(a)
    b_high, b_low = split(b)
    return mm(
        jnp.concatenate([a_high, a_high, a_low], axis=1), jnp.concatenate([b_high, b_low, b_high], axis=0)
    )


def fourth_kernel(left_ref, right_ref, left_out, right_out):
    for ref, out in ((left_ref, left_out), (right_ref, right_out)):
        root = ref[0, 0]
        square = dot3(root, root)
        out[0, 0] = dot3(square, square)


def fourth_powers(left_root, right_root):
    slabs, col_blocks, order, _ = left_root.shape
    spec = pl.BlockSpec((1, 1, order, order), lambda i, j: (i, j, 0, 0))
    shape = jax.ShapeDtypeStruct(left_root.shape, jnp.float32)
    count = slabs * col_blocks
    return pl.pallas_call(
        fourth_kernel,
        grid=(slabs, col_blocks),
        in_specs=[spec, spec],
        out_specs=[spec, spec],
        out_shape=[shape, shape],
        compiler_params=pltpu.CompilerParams(vmem_limit_bytes=VMEM_LIMIT),
        cost_estimate=pl.CostEstimate(
            flops=count * 4 * 3 * 2 * order**3, bytes_accessed=count * 16 * order**2, transcendentals=0
        ),
        name="fourth_powers",
    )(left_root, right_root)


def slab_of(k, e, outer_place, inner_place, inner):
    return (outer_place ^ k) * inner + (inner_place ^ e)


def pack_kernel(ranks, inner, place_ref, grads_ref, out_ref):
    d = pl.program_id(0)
    for k in range(ranks):
        for e in range(inner):
            out_ref[0, k * inner + e, 0] = grads_ref[slab_of(k, e, d, place_ref[1], inner), 0]


def pack(ranks, inner, slots, per, place, grads):
    first, count = slots
    slabs, order, width = grads.shape
    owners, rows = slabs // per, order // ranks
    packed = pl.pallas_call(
        functools.partial(pack_kernel, ranks, inner),
        grid=(ranks, count),
        in_specs=[
            pl.BlockSpec(memory_space=pltpu.SMEM),
            pl.BlockSpec((owners, 1, rows, width), lambda d, s: (0, first + s, d, 0)),
        ],
        out_specs=pl.BlockSpec((1, owners, 1, rows, width), lambda d, s: (d, 0, s, 0, 0)),
        out_shape=jax.ShapeDtypeStruct((ranks, owners, count, rows, width), grads.dtype),
        compiler_params=pltpu.CompilerParams(vmem_limit_bytes=VMEM_LIMIT),
        cost_estimate=pl.CostEstimate(
            flops=0, bytes_accessed=4 * owners * count * order * width, transcendentals=0
        ),
        name="pack_slabs",
    )(place, grads.reshape(owners, per, order, width))
    return packed.reshape(-1, width)


def unpack_kernel(ranks, inner, place_ref, got_ref, *rest):
    out_ref = rest[-1]
    for k in range(ranks):
        for e in range(inner):
            slab = slab_of(k, e, place_ref[0], place_ref[1], inner)
            out_ref[slab, 0] = got_ref[0, k * inner + e, 0]


def unpack(ranks, inner, slots, per, place, got, so_far):
    first, count = slots
    width, owners = got.shape[1], ranks * inner
    rows = got.shape[0] // (ranks * owners * count)
    operands = [place, got.reshape(ranks, owners, count, rows, width)]
    operands += [] if so_far is None else [so_far]
    return pl.pallas_call(
        functools.partial(unpack_kernel, ranks, inner),
        grid=(ranks, count),
        in_specs=[
            pl.BlockSpec(memory_space=pltpu.SMEM),
            pl.BlockSpec((1, owners, 1, rows, width), lambda d, s: (d, 0, s, 0, 0)),
        ]
        + [pl.BlockSpec(memory_space=pl.ANY)] * (len(operands) - 2),
        out_specs=pl.BlockSpec((owners, 1, rows, width), lambda d, s: (0, first + s, d, 0)),
        out_shape=jax.ShapeDtypeStruct((owners, per, ranks * rows, width), got.dtype),
        input_output_aliases={} if so_far is None else {2: 0},
        compiler_params=pltpu.CompilerParams(vmem_limit_bytes=VMEM_LIMIT),
        cost_estimate=pl.CostEstimate(flops=0, bytes_accessed=4 * got.size, transcendentals=0),
        name="unpack_slabs",
    )(*operands)


def route_kernel(ranks, inner, count, place_ref, *refs):
    taken, outs, held = refs[:ranks], refs[ranks:-1], refs[-1]
    rows = outs[0].shape[0] // count
    turn, inner_place = place_ref[2] ^ place_ref[0], place_ref[1]
    for k in range(ranks):
        held[k] = taken[k][...]
    for m in range(ranks):
        for e in range(inner):
            for s in range(count):
                start = pl.multiple_of((s * inner + (inner_place ^ e)) * rows, rows)
                outs[m * inner + e][s * rows : (s + 1) * rows] = held[turn ^ m, pl.ds(start, rows), :]


def route(ranks, inner, count, place, taken):
    rows, width = taken[0].shape[0] // inner, taken[0].shape[1]
    vmem = pl.BlockSpec(memory_space=pltpu.VMEM)
    return pl.pallas_call(
        functools.partial(route_kernel, ranks, inner, count),
        in_specs=[pl.BlockSpec(memory_space=pltpu.SMEM)] + [vmem] * ranks,
        out_specs=[vmem] * (ranks * inner),
        out_shape=[jax.ShapeDtypeStruct((rows, width), taken[0].dtype)] * (ranks * inner),
        scratch_shapes=[pltpu.VMEM((ranks, inner * rows, width), taken[0].dtype)],
        compiler_params=pltpu.CompilerParams(vmem_limit_bytes=VMEM_LIMIT // 4),
        cost_estimate=pl.CostEstimate(
            flops=0, bytes_accessed=4 * ranks * taken[0].size, transcendentals=0
        ),
        name="route",
    )(place, *taken)


def refine(root, fourth, stats):
    order = root.shape[0]
    coupled = dot3(fourth, stats)
    on_diagonal = lax.broadcasted_iota(jnp.int32, (order, order), 0) == lax.broadcasted_iota(
        jnp.int32, (order, order), 1
    )
    factor = (jnp.where(on_diagonal, 5.0, 0.0) - coupled) * 0.25
    return dot3(root, factor)


def block_kernel(ranks, inner, steps, place_ref, *refs):
    count = ranks * inner
    pieces = refs[:count]
    left_stats, right_stats, left_root, right_root, left_fourth, right_fourth = refs[count : count + 6]
    outs = refs[count + 6 : count + 6 + ranks]
    blocks, results = refs[count + 6 + ranks :]
    rows, width = pieces[0].shape
    order = blocks.shape[1]
    outer_place, inner_place = place_ref[0], place_ref[1]
    step = pl.program_id(1)
    per_block = order // width

    def spot(rank, shard):
        row = pl.multiple_of(rank * rows, rows)
        column = pl.multiple_of((shard % per_block) * width, width)
        return shard // per_block, pl.ds(row, rows), pl.ds(column, width)

    @pl.when(step == 0)
    def _():
        for k in range(ranks):
            for e in range(inner):
                blocks[spot(outer_place ^ k, inner_place ^ e)] = pieces[k * inner + e][...]

    block = blocks[step]
    turned = block.T
    left = ema_decay * left_stats[0, 0] + (1.0 - ema_decay) * mm(block, turned)
    right = ema_decay * right_stats[0, 0] + (1.0 - ema_decay) * mm(turned, block)
    new_left = refine(left_root[0, 0], left_fourth[0, 0], left)
    new_right = refine(right_root[0, 0], right_fourth[0, 0], right)
    high, low = split(new_left)
    halfway = mm(high, block) + mm(low, block)
    results[step] = dot3(halfway, new_right).astype(results.dtype)

    @pl.when(step == steps - 1)
    def _():
        for k in range(ranks):
            for b in range(inner):
                outs[k][b * rows : (b + 1) * rows] = results[spot(place_ref[2] ^ k, b)]


def precondition(ranks, inner, slots, place, pieces, stats_and_roots):
    first, count = slots
    _, col_blocks, order, _ = stats_and_roots[0].shape
    rows, width = pieces[0].shape[0] // count, pieces[0].shape[1]
    owners = ranks * inner
    piece = pl.BlockSpec((rows, width), lambda s, j: (s, 0))
    strip = pl.BlockSpec((inner * rows, width), lambda s, j: (s, 0))
    matrix = pl.BlockSpec((1, 1, order, order), lambda s, j: (first + s, j, 0, 0))
    return pl.pallas_call(
        functools.partial(block_kernel, ranks, inner, col_blocks),
        grid=(count, col_blocks),
        in_specs=[pl.BlockSpec(memory_space=pltpu.SMEM)] + [piece] * owners + [matrix] * 6,
        out_specs=[strip] * ranks,
        out_shape=[jax.ShapeDtypeStruct((count * inner * rows, width), jnp.bfloat16)] * ranks,
        scratch_shapes=[pltpu.VMEM((col_blocks, order, order), jnp.bfloat16)] * 2,
        compiler_params=pltpu.CompilerParams(vmem_limit_bytes=VMEM_LIMIT * 2 // 3),
        cost_estimate=pl.CostEstimate(
            flops=count * col_blocks * 19 * 2 * order**3,
            bytes_accessed=count * col_blocks * 28 * order**2,
            transcendentals=0,
        ),
        name="precondition",
    )(place, *pieces, *stats_and_roots)


def shards(ranks, fsdp, grads, left_stats, right_stats, left_root, right_root):
    per = left_stats.shape[0]
    inner = fsdp // ranks
    grads = grads[0]
    slabs, order, width = grads.shape
    rows = order // ranks
    f = lax.axis_index("fsdp")
    place = jnp.stack([f // inner, f % inner, lax.axis_index("dp")]).astype(jnp.int32)
    rounds = [(k, e) for k in range(ranks) for e in range(inner)]

    def number(d, a, b):
        return (d * ranks + a) * inner + b

    sources = [(d, a, b) for d in range(ranks) for a in range(ranks) for b in range(inner)]
    to_owner = {
        (k, e): [(number(d, a, b), number(a, d ^ k, b ^ e)) for d, a, b in sources] for k, e in rounds
    }
    to_row = [[(d, d ^ k) for d in range(ranks)] for k in range(ranks)]
    to_column = {
        (m, e): [(a * inner + b, (a ^ m) * inner + (b ^ e)) for a in range(ranks) for b in range(inner)]
        for m, e in rounds
    }

    half = max(per // 2, 1)
    groups = [(first, min(half, per - first)) for first in range(0, per, half)]
    summed = []
    for slots in groups:
        packed = pack(ranks, inner, slots, per, place, grads)
        summed.append(lax.psum_scatter(packed, "dp", scatter_dimension=0, tiled=True))
    left_fourth, right_fourth = fourth_powers(left_root, right_root)
    summed[0], left_fourth, right_fourth = lax.optimization_barrier((summed[0], left_fourth, right_fourth))
    matrices = (left_stats, right_stats, left_root, right_root, left_fourth, right_fourth)

    def send_in(g):
        size = groups[g][1] * rows
        return [
            lax.ppermute(summed[g][at * size : (at + 1) * size], MESH_AXES, to_owner[key])
            for at, key in enumerate(rounds)
        ]

    def work(g, arrived):
        return precondition(ranks, inner, groups[g], place, arrived, matrices)

    strips = work(0, send_in(0))
    out = None
    for g, slots in enumerate(groups):
        last = g + 1 == len(groups)
        if not last:
            summed[g + 1], held = lax.optimization_barrier((summed[g + 1], strips[0]))
            strips = [held] + list(strips[1:])
        moved = [strips[0]] + [lax.ppermute(strips[k], "dp", to_row[k]) for k in range(1, ranks)]
        if not last:
            moved, arrived = lax.optimization_barrier((moved, send_in(g + 1)))
        routed = route(ranks, inner, slots[1], place, moved)
        back = [routed[0]] + [
            lax.ppermute(piece, "fsdp", to_column[key]) for piece, key in zip(routed[1:], rounds[1:])
        ]
        if not last:
            back, strips = lax.optimization_barrier((back, work(g + 1, arrived)))
        gathered = lax.all_gather(jnp.concatenate(back, axis=0), "dp", axis=0, tiled=True)
        out = unpack(ranks, inner, slots, per, place, gathered, out)
    return out.reshape(grads.shape)


def solution(mesh):
    placed = (
        P("dp", None, None, "fsdp"),
        P("fsdp", "dp", None, None),
        P("fsdp", "dp", None, None),
        P("fsdp", "dp", None, None),
        P("fsdp", "dp", None, None),
    )
    run = functools.partial(shards, mesh.shape["dp"], mesh.shape["fsdp"])
    return jax.shard_map(
        run, mesh=mesh, in_specs=placed, out_specs=P(None, None, "fsdp"), check_vma=False
    )
```

```python
import functools

import jax
import jax.numpy as jnp
from jax import lax
from jax.experimental import pallas as pl
from jax.experimental.pallas import tpu as pltpu
from jax.sharding import PartitionSpec as P

ema_decay = 0.999
MESH_AXES = ("dp", "fsdp")
VMEM_LIMIT = 60 * 1024 * 1024


def split(x):
    high = x.astype(jnp.bfloat16)
    low = (x - high.astype(jnp.float32)).astype(jnp.bfloat16)
    return high, low


def mm(a, b):
    return jnp.dot(a, b, preferred_element_type=jnp.float32)


def dot3(a, b):
    a_high, a_low = split(a)
    b_high, b_low = split(b)
    return mm(
        jnp.concatenate([a_high, a_high, a_low], axis=1), jnp.concatenate([b_high, b_low, b_high], axis=0)
    )


def fourth_kernel(left_ref, right_ref, left_out, right_out):
    for ref, out in ((left_ref, left_out), (right_ref, right_out)):
        root = ref[0, 0]
        square = dot3(root, root)
        out[0, 0] = dot3(square, square)


def fourth_powers(left_root, right_root):
    slabs, col_blocks, order, _ = left_root.shape
    spec = pl.BlockSpec((1, 1, order, order), lambda i, j: (i, j, 0, 0))
    shape = jax.ShapeDtypeStruct(left_root.shape, jnp.float32)
    count = slabs * col_blocks
    return pl.pallas_call(
        fourth_kernel,
        grid=(slabs, col_blocks),
        in_specs=[spec, spec],
        out_specs=[spec, spec],
        out_shape=[shape, shape],
        compiler_params=pltpu.CompilerParams(vmem_limit_bytes=VMEM_LIMIT),
        cost_estimate=pl.CostEstimate(
            flops=count * 4 * 3 * 2 * order**3, bytes_accessed=count * 16 * order**2, transcendentals=0
        ),
        name="fourth_powers",
    )(left_root, right_root)


def slab_of(k, e, outer_place, inner_place, inner):
    return (outer_place ^ k) * inner + (inner_place ^ e)


def pack_kernel(ranks, inner, place_ref, grads_ref, out_ref):
    d = pl.program_id(0)
    for k in range(ranks):
        for e in range(inner):
            slab = slab_of(k, e, d ^ place_ref[0], place_ref[1], inner)
            out_ref[0, 0, k * inner + e] = grads_ref[slab, 0]


def pack(ranks, inner, slots, per, place, grads):
    first, count = slots
    slabs, order, width = grads.shape
    owners, rows = slabs // per, order // ranks
    packed = pl.pallas_call(
        functools.partial(pack_kernel, ranks, inner),
        grid=(ranks, count),
        in_specs=[
            pl.BlockSpec(memory_space=pltpu.SMEM),
            pl.BlockSpec((owners, 1, rows, width), lambda d, s: (0, first + s, d, 0)),
        ],
        out_specs=pl.BlockSpec((1, 1, owners, rows, width), lambda d, s: (d, s, 0, 0, 0)),
        out_shape=jax.ShapeDtypeStruct((ranks, count, owners, rows, width), grads.dtype),
        compiler_params=pltpu.CompilerParams(vmem_limit_bytes=VMEM_LIMIT),
        cost_estimate=pl.CostEstimate(
            flops=0, bytes_accessed=4 * owners * count * order * width, transcendentals=0
        ),
        name="pack_slabs",
    )(place, grads.reshape(owners, per, order, width))
    return packed.reshape(-1, width)


def unpack_kernel(ranks, inner, place_ref, got_ref, *rest):
    out_ref = rest[-1]
    for k in range(ranks):
        for e in range(inner):
            slab = slab_of(k, e, place_ref[0], place_ref[1], inner)
            out_ref[slab, 0] = got_ref[0, 0, k * inner + e]


def unpack(ranks, inner, slots, per, place, got, so_far):
    first, count = slots
    width, owners = got.shape[1], ranks * inner
    rows = got.shape[0] // (ranks * owners * count)
    operands = [place, got.reshape(ranks, count, owners, rows, width)]
    operands += [] if so_far is None else [so_far]
    return pl.pallas_call(
        functools.partial(unpack_kernel, ranks, inner),
        grid=(ranks, count),
        in_specs=[
            pl.BlockSpec(memory_space=pltpu.SMEM),
            pl.BlockSpec((1, 1, owners, rows, width), lambda d, s: (d, s, 0, 0, 0)),
        ]
        + [pl.BlockSpec(memory_space=pl.ANY)] * (len(operands) - 2),
        out_specs=pl.BlockSpec((owners, 1, rows, width), lambda d, s: (0, first + s, d, 0)),
        out_shape=jax.ShapeDtypeStruct((owners, per, ranks * rows, width), got.dtype),
        input_output_aliases={} if so_far is None else {2: 0},
        compiler_params=pltpu.CompilerParams(vmem_limit_bytes=VMEM_LIMIT),
        cost_estimate=pl.CostEstimate(flops=0, bytes_accessed=4 * got.size, transcendentals=0),
        name="unpack_slabs",
    )(*operands)


def route_kernel(ranks, inner, place_ref, *refs):
    taken, outs, held = refs[:ranks], refs[ranks:-1], refs[-1]
    rows = outs[0].shape[0]
    turn, inner_place = place_ref[2] ^ place_ref[0], place_ref[1]
    for k in range(ranks):
        held[k] = taken[k][...]
    for m in range(ranks):
        for e in range(inner):
            start = pl.multiple_of((inner_place ^ e) * rows, rows)
            outs[m * inner + e][...] = held[turn ^ m, pl.ds(start, rows), :]


def route(ranks, inner, place, taken):
    rows, width = taken[0].shape[0] // inner, taken[0].shape[1]
    vmem = pl.BlockSpec(memory_space=pltpu.VMEM)
    return pl.pallas_call(
        functools.partial(route_kernel, ranks, inner),
        in_specs=[pl.BlockSpec(memory_space=pltpu.SMEM)] + [vmem] * ranks,
        out_specs=[vmem] * (ranks * inner),
        out_shape=[jax.ShapeDtypeStruct((rows, width), taken[0].dtype)] * (ranks * inner),
        scratch_shapes=[pltpu.VMEM((ranks, inner * rows, width), taken[0].dtype)],
        compiler_params=pltpu.CompilerParams(vmem_limit_bytes=VMEM_LIMIT // 4),
        cost_estimate=pl.CostEstimate(
            flops=0, bytes_accessed=4 * ranks * taken[0].size, transcendentals=0
        ),
        name="route",
    )(place, *taken)


def refine(root, fourth, stats):
    order = root.shape[0]
    coupled = dot3(fourth, stats)
    on_diagonal = lax.broadcasted_iota(jnp.int32, (order, order), 0) == lax.broadcasted_iota(
        jnp.int32, (order, order), 1
    )
    factor = (jnp.where(on_diagonal, 5.0, 0.0) - coupled) * 0.25
    return dot3(root, factor)


def block_kernel(ranks, inner, steps, place_ref, *refs):
    count = ranks * inner
    pieces = refs[:count]
    left_stats, right_stats, left_root, right_root, left_fourth, right_fourth = refs[count : count + 6]
    outs = refs[count + 6 : count + 6 + ranks]
    blocks, results = refs[count + 6 + ranks :]
    rows, width = pieces[0].shape
    order = blocks.shape[1]
    outer_place, inner_place = place_ref[0], place_ref[1]
    step = pl.program_id(0)
    per_block = order // width

    def spot(rank, shard):
        row = pl.multiple_of(rank * rows, rows)
        column = pl.multiple_of((shard % per_block) * width, width)
        return shard // per_block, pl.ds(row, rows), pl.ds(column, width)

    @pl.when(step == 0)
    def _():
        for k in range(ranks):
            for e in range(inner):
                blocks[spot(place_ref[2] ^ outer_place ^ k, inner_place ^ e)] = pieces[k * inner + e][...]

    block = blocks[step]
    turned = block.T
    left = ema_decay * left_stats[0, 0] + (1.0 - ema_decay) * mm(block, turned)
    right = ema_decay * right_stats[0, 0] + (1.0 - ema_decay) * mm(turned, block)
    new_left = refine(left_root[0, 0], left_fourth[0, 0], left)
    new_right = refine(right_root[0, 0], right_fourth[0, 0], right)
    high, low = split(new_left)
    halfway = mm(high, block) + mm(low, block)
    results[step] = dot3(halfway, new_right).astype(results.dtype)

    @pl.when(step == steps - 1)
    def _():
        for k in range(ranks):
            for b in range(inner):
                outs[k][b * rows : (b + 1) * rows] = results[spot(place_ref[2] ^ k, b)]


def precondition(ranks, inner, slot, place, pieces, stats_and_roots):
    _, col_blocks, order, _ = stats_and_roots[0].shape
    rows, width = pieces[0].shape
    owners = ranks * inner
    piece = pl.BlockSpec((rows, width), lambda j: (0, 0))
    strip = pl.BlockSpec((inner * rows, width), lambda j: (0, 0))
    matrix = pl.BlockSpec((1, 1, order, order), lambda j: (slot, j, 0, 0))
    return pl.pallas_call(
        functools.partial(block_kernel, ranks, inner, col_blocks),
        grid=(col_blocks,),
        in_specs=[pl.BlockSpec(memory_space=pltpu.SMEM)] + [piece] * owners + [matrix] * 6,
        out_specs=[strip] * ranks,
        out_shape=[jax.ShapeDtypeStruct((inner * rows, width), jnp.bfloat16)] * ranks,
        scratch_shapes=[pltpu.VMEM((col_blocks, order, order), jnp.bfloat16)] * 2,
        compiler_params=pltpu.CompilerParams(vmem_limit_bytes=VMEM_LIMIT * 9 // 10),
        cost_estimate=pl.CostEstimate(
            flops=col_blocks * 19 * 2 * order**3,
            bytes_accessed=col_blocks * 28 * order**2,
            transcendentals=0,
        ),
        name="precondition",
    )(place, *pieces, *stats_and_roots)


def shards(ranks, fsdp, grads, left_stats, right_stats, left_root, right_root):
    per = left_stats.shape[0]
    inner = fsdp // ranks
    grads = grads[0]
    slabs, order, width = grads.shape
    rows = order // ranks
    f = lax.axis_index("fsdp")
    place = jnp.stack([f // inner, f % inner, lax.axis_index("dp")]).astype(jnp.int32)
    rounds = [(k, e) for k in range(ranks) for e in range(inner)]

    def number(d, a, b):
        return (d * ranks + a) * inner + b

    sources = [(d, a, b) for d in range(ranks) for a in range(ranks) for b in range(inner)]
    to_owner = {
        (k, e): [(number(d, a, b), number(a, d ^ a ^ k, b ^ e)) for d, a, b in sources] for k, e in rounds
    }
    to_row = [[(d, d ^ k) for d in range(ranks)] for k in range(ranks)]
    to_column = {
        (m, e): [(a * inner + b, (a ^ m) * inner + (b ^ e)) for a in range(ranks) for b in range(inner)]
        for m, e in rounds
    }

    half = max(per // 2, 1)
    groups = [(first, min(half, per - first)) for first in range(0, per, half)]
    summed = []
    for slots in groups:
        packed = pack(ranks, inner, slots, per, place, grads)
        summed.append(lax.psum_scatter(packed, "dp", scatter_dimension=0, tiled=True))
    left_fourth, right_fourth = fourth_powers(left_root, right_root)
    summed[0], left_fourth, right_fourth = lax.optimization_barrier((summed[0], left_fourth, right_fourth))
    matrices = (left_stats, right_stats, left_root, right_root, left_fourth, right_fourth)

    piece_count = len(rounds)

    def send_in(slot):
        g, s = divmod(slot, half)
        pieces = summed[g].reshape(-1, rows, width)[s * piece_count : (s + 1) * piece_count]
        return [lax.ppermute(pieces[at], MESH_AXES, to_owner[key]) for at, key in enumerate(rounds)]

    def work(slot, arrived):
        return precondition(ranks, inner, slot, place, arrived, matrices)

    def send_rows(slot, strips):
        return [strips[0]] + [lax.ppermute(strips[k], "dp", to_row[k]) for k in range(1, ranks)]

    def send_columns(slot, moved):
        routed = route(ranks, inner, place, moved)
        return [routed[0]] + [
            lax.ppermute(piece, "fsdp", to_column[key]) for piece, key in zip(routed[1:], rounds[1:])
        ]

    stages = (send_in, work, send_rows, send_columns)
    begins = [slot + (slot // half) * (len(stages) - 1) for slot in range(per)]
    held = {}
    out = None
    for tick in range(begins[-1] + len(stages)):
        now = {}
        for slot, begin in enumerate(begins):
            stage = tick - begin
            if stage == 0:
                now[slot] = send_in(slot)
            elif 0 < stage < len(stages):
                now[slot] = stages[stage](slot, held[slot])
        wanted = [begins.index(tick + 1) // half] if tick + 1 in begins else []
        now, ahead = lax.optimization_barrier((now, [summed[g] for g in wanted]))
        for g, value in zip(wanted, ahead):
            summed[g] = value
        held.update(now)
        for g, (first, count) in enumerate(groups):
            if begins[first + count - 1] + len(stages) - 1 == tick:
                back = [piece for slot in range(first, first + count) for piece in held[slot]]
                gathered = lax.all_gather(jnp.concatenate(back, axis=0), "dp", axis=0, tiled=True)
                out = unpack(ranks, inner, (first, count), per, place, gathered, out)
    return out.reshape(grads.shape)


def solution(mesh):
    placed = (
        P("dp", None, None, "fsdp"),
        P("fsdp", "dp", None, None),
        P("fsdp", "dp", None, None),
        P("fsdp", "dp", None, None),
        P("fsdp", "dp", None, None),
    )
    run = functools.partial(shards, mesh.shape["dp"], mesh.shape["fsdp"])
    return jax.shard_map(
        run, mesh=mesh, in_specs=placed, out_specs=P(None, None, "fsdp"), check_vma=False
    )
```

```python
import functools

import jax
import jax.numpy as jnp
from jax import lax
from jax.experimental import pallas as pl
from jax.experimental.pallas import tpu as pltpu
from jax.sharding import PartitionSpec as P

ema_decay = 0.999
MESH_AXES = ("dp", "fsdp")
VMEM_LIMIT = 60 * 1024 * 1024


def split(x):
    high = x.astype(jnp.bfloat16)
    low = (x - high.astype(jnp.float32)).astype(jnp.bfloat16)
    return high, low


def mm(a, b):
    return jnp.dot(a, b, preferred_element_type=jnp.float32)


def dot3(a, b):
    a_high, a_low = split(a)
    b_high, b_low = split(b)
    return mm(
        jnp.concatenate([a_high, a_high, a_low], axis=1), jnp.concatenate([b_high, b_low, b_high], axis=0)
    )


def fourth_kernel(left_ref, right_ref, left_out, right_out):
    for ref, out in ((left_ref, left_out), (right_ref, right_out)):
        root = ref[0, 0]
        square = dot3(root, root)
        out[0, 0] = dot3(square, square)


def fourth_powers(left_root, right_root):
    slabs, col_blocks, order, _ = left_root.shape
    spec = pl.BlockSpec((1, 1, order, order), lambda i, j: (i, j, 0, 0))
    shape = jax.ShapeDtypeStruct(left_root.shape, jnp.float32)
    count = slabs * col_blocks
    return pl.pallas_call(
        fourth_kernel,
        grid=(slabs, col_blocks),
        in_specs=[spec, spec],
        out_specs=[spec, spec],
        out_shape=[shape, shape],
        compiler_params=pltpu.CompilerParams(vmem_limit_bytes=VMEM_LIMIT),
        cost_estimate=pl.CostEstimate(
            flops=count * 4 * 3 * 2 * order**3, bytes_accessed=count * 16 * order**2, transcendentals=0
        ),
        name="fourth_powers",
    )(left_root, right_root)


def slab_of(k, e, outer_place, inner_place, inner):
    return (outer_place ^ k) * inner + (inner_place ^ e)


def pack_kernel(ranks, inner, place_ref, grads_ref, out_ref):
    d = pl.program_id(0)
    for k in range(ranks):
        for e in range(inner):
            slab = slab_of(k, e, d ^ place_ref[0], place_ref[1], inner)
            out_ref[0, e, 0, k] = grads_ref[slab, 0]


def pack(ranks, inner, slots, per, place, grads):
    first, count = slots
    slabs, order, width = grads.shape
    owners, rows = slabs // per, order // ranks
    packed = pl.pallas_call(
        functools.partial(pack_kernel, ranks, inner),
        grid=(ranks, count),
        in_specs=[
            pl.BlockSpec(memory_space=pltpu.SMEM),
            pl.BlockSpec((owners, 1, rows, width), lambda d, s: (0, first + s, d, 0)),
        ],
        out_specs=pl.BlockSpec((1, inner, 1, ranks, rows, width), lambda d, s: (d, 0, s, 0, 0, 0)),
        out_shape=jax.ShapeDtypeStruct((ranks, inner, count, ranks, rows, width), grads.dtype),
        compiler_params=pltpu.CompilerParams(vmem_limit_bytes=VMEM_LIMIT),
        cost_estimate=pl.CostEstimate(
            flops=0, bytes_accessed=4 * owners * count * order * width, transcendentals=0
        ),
        name="pack_slabs",
    )(place, grads.reshape(owners, per, order, width))
    return packed.reshape(-1, width)


def unpack_kernel(ranks, inner, place_ref, got_ref, *rest):
    out_ref = rest[-1]
    for k in range(ranks):
        for e in range(inner):
            slab = slab_of(k, e, place_ref[0], place_ref[1], inner)
            out_ref[slab, 0] = got_ref[0, 0, k * inner + e]


def unpack(ranks, inner, slots, per, place, got, so_far):
    first, count = slots
    width, owners = got.shape[1], ranks * inner
    rows = got.shape[0] // (ranks * owners * count)
    operands = [place, got.reshape(ranks, count, owners, rows, width)]
    operands += [] if so_far is None else [so_far]
    return pl.pallas_call(
        functools.partial(unpack_kernel, ranks, inner),
        grid=(ranks, count),
        in_specs=[
            pl.BlockSpec(memory_space=pltpu.SMEM),
            pl.BlockSpec((1, 1, owners, rows, width), lambda d, s: (d, s, 0, 0, 0)),
        ]
        + [pl.BlockSpec(memory_space=pl.ANY)] * (len(operands) - 2),
        out_specs=pl.BlockSpec((owners, 1, rows, width), lambda d, s: (0, first + s, d, 0)),
        out_shape=jax.ShapeDtypeStruct((owners, per, ranks * rows, width), got.dtype),
        input_output_aliases={} if so_far is None else {2: 0},
        compiler_params=pltpu.CompilerParams(vmem_limit_bytes=VMEM_LIMIT),
        cost_estimate=pl.CostEstimate(flops=0, bytes_accessed=4 * got.size, transcendentals=0),
        name="unpack_slabs",
    )(*operands)


def route_kernel(ranks, inner, place_ref, *refs):
    taken, outs, held = refs[:ranks], refs[ranks:-1], refs[-1]
    rows = outs[0].shape[0]
    turn, inner_place = place_ref[2] ^ place_ref[0], place_ref[1]
    for k in range(ranks):
        held[k] = taken[k][...]
    for m in range(ranks):
        for e in range(inner):
            start = pl.multiple_of((inner_place ^ e) * rows, rows)
            outs[m * inner + e][...] = held[turn ^ m, pl.ds(start, rows), :]


def route(ranks, inner, place, taken):
    rows, width = taken[0].shape[0] // inner, taken[0].shape[1]
    vmem = pl.BlockSpec(memory_space=pltpu.VMEM)
    return pl.pallas_call(
        functools.partial(route_kernel, ranks, inner),
        in_specs=[pl.BlockSpec(memory_space=pltpu.SMEM)] + [vmem] * ranks,
        out_specs=[vmem] * (ranks * inner),
        out_shape=[jax.ShapeDtypeStruct((rows, width), taken[0].dtype)] * (ranks * inner),
        scratch_shapes=[pltpu.VMEM((ranks, inner * rows, width), taken[0].dtype)],
        compiler_params=pltpu.CompilerParams(vmem_limit_bytes=VMEM_LIMIT // 4),
        cost_estimate=pl.CostEstimate(
            flops=0, bytes_accessed=4 * ranks * taken[0].size, transcendentals=0
        ),
        name="route",
    )(place, *taken)


def refine(root, fourth, stats):
    order = root.shape[0]
    coupled = dot3(fourth, stats)
    on_diagonal = lax.broadcasted_iota(jnp.int32, (order, order), 0) == lax.broadcasted_iota(
        jnp.int32, (order, order), 1
    )
    factor = (jnp.where(on_diagonal, 5.0, 0.0) - coupled) * 0.25
    return dot3(root, factor)


def block_kernel(ranks, inner, steps, place_ref, *refs):
    pieces = refs[:ranks]
    left_stats, right_stats, left_root, right_root, left_fourth, right_fourth = refs[ranks : ranks + 6]
    outs = refs[ranks + 6 : 2 * ranks + 6]
    blocks, results = refs[2 * ranks + 6 :]
    rows, width = pieces[0].shape[0] // inner, pieces[0].shape[1]
    order = blocks.shape[1]
    outer_place, inner_place = place_ref[0], place_ref[1]
    step = pl.program_id(0)
    per_block = order // width

    def spot(rank, shard):
        row = pl.multiple_of(rank * rows, rows)
        column = pl.multiple_of((shard % per_block) * width, width)
        return shard // per_block, pl.ds(row, rows), pl.ds(column, width)

    @pl.when(step == 0)
    def _():
        for k in range(ranks):
            for e in range(inner):
                blocks[spot(place_ref[2] ^ outer_place ^ k, inner_place ^ e)] = pieces[k][e * rows : (e + 1) * rows]

    block = blocks[step]
    turned = block.T
    left = ema_decay * left_stats[0, 0] + (1.0 - ema_decay) * mm(block, turned)
    right = ema_decay * right_stats[0, 0] + (1.0 - ema_decay) * mm(turned, block)
    new_left = refine(left_root[0, 0], left_fourth[0, 0], left)
    new_right = refine(right_root[0, 0], right_fourth[0, 0], right)
    halfway = mm(new_left.astype(jnp.bfloat16), block)
    results[step] = mm(halfway.astype(jnp.bfloat16), new_right.astype(jnp.bfloat16)).astype(results.dtype)

    @pl.when(step == steps - 1)
    def _():
        for k in range(ranks):
            for b in range(inner):
                outs[k][b * rows : (b + 1) * rows] = results[spot(place_ref[2] ^ k, b)]


def precondition(ranks, inner, slot, place, pieces, stats_and_roots):
    _, col_blocks, order, _ = stats_and_roots[0].shape
    strip = pl.BlockSpec(pieces[0].shape, lambda j: (0, 0))
    matrix = pl.BlockSpec((1, 1, order, order), lambda j: (slot, j, 0, 0))
    return pl.pallas_call(
        functools.partial(block_kernel, ranks, inner, col_blocks),
        grid=(col_blocks,),
        in_specs=[pl.BlockSpec(memory_space=pltpu.SMEM)] + [strip] * ranks + [matrix] * 6,
        out_specs=[strip] * ranks,
        out_shape=[jax.ShapeDtypeStruct(pieces[0].shape, jnp.bfloat16)] * ranks,
        scratch_shapes=[pltpu.VMEM((col_blocks, order, order), jnp.bfloat16)] * 2,
        compiler_params=pltpu.CompilerParams(vmem_limit_bytes=VMEM_LIMIT * 9 // 10),
        cost_estimate=pl.CostEstimate(
            flops=col_blocks * 16 * 2 * order**3,
            bytes_accessed=col_blocks * 28 * order**2,
            transcendentals=0,
        ),
        name="precondition",
    )(place, *pieces, *stats_and_roots)


def shards(ranks, fsdp, grads, left_stats, right_stats, left_root, right_root):
    per = left_stats.shape[0]
    inner = fsdp // ranks
    grads = grads[0]
    slabs, order, width = grads.shape
    rows = order // ranks
    f = lax.axis_index("fsdp")
    place = jnp.stack([f // inner, f % inner, lax.axis_index("dp")]).astype(jnp.int32)
    rounds = [(k, e) for k in range(ranks) for e in range(inner)]

    def number(d, a, b):
        return (d * ranks + a) * inner + b

    sources = [(d, a, b) for d in range(ranks) for a in range(ranks) for b in range(inner)]
    to_core = [
        [(a * inner + b, a * inner + (b ^ e)) for a in range(ranks) for b in range(inner)] for e in range(inner)
    ]
    to_owner = [
        [(number(d, a, b), number(a, d ^ a ^ k, b)) for d, a, b in sources] for k in range(ranks)
    ]
    to_row = [[(d, d ^ k) for d in range(ranks)] for k in range(ranks)]
    to_column = {
        (m, e): [(a * inner + b, (a ^ m) * inner + (b ^ e)) for a in range(ranks) for b in range(inner)]
        for m, e in rounds
    }

    half = max(per // 2, 1)
    sums = [(0, half)] + [(slot, 1) for slot in range(half, per)]
    gathers = [(first, min(half, per - first)) for first in range(0, per, half)]
    begins = [slot if slot < half else half + 1 + 2 * (slot - half) for slot in range(per)]
    group_of = [max(g for g, (first, _) in enumerate(sums) if first <= slot) for slot in range(per)]
    ready = []
    for slots in sums:
        packed = pack(ranks, inner, slots, per, place, grads)
        ready.append([lax.psum_scatter(packed, "dp", scatter_dimension=0, tiled=True)])
    left_fourth, right_fourth = fourth_powers(left_root, right_root)
    ready[0], left_fourth, right_fourth = lax.optimization_barrier((ready[0], left_fourth, right_fourth))
    matrices = (left_stats, right_stats, left_root, right_root, left_fourth, right_fourth)

    def between_cores(g):
        parts = ready[g][0].reshape(inner, -1, width)
        ready[g] = [parts[0]] + [lax.ppermute(parts[e], "fsdp", to_core[e]) for e in range(1, inner)]

    def send_in(slot):
        g = group_of[slot]
        if slot == sums[g][0]:
            between_cores(g)
        at = (slot - sums[g][0]) * ranks
        strips = [
            jnp.concatenate([part[(at + k) * rows : (at + k + 1) * rows] for part in ready[g]], axis=0)
            for k in range(ranks)
        ]
        return [lax.ppermute(strips[k], MESH_AXES, to_owner[k]) for k in range(ranks)]

    def work(slot, arrived):
        return precondition(ranks, inner, slot, place, arrived, matrices)

    def send_rows(slot, strips):
        return [strips[0]] + [lax.ppermute(strips[k], "dp", to_row[k]) for k in range(1, ranks)]

    def send_columns(slot, moved):
        routed = route(ranks, inner, place, moved)
        return [routed[0]] + [
            lax.ppermute(piece, "fsdp", to_column[key]) for piece, key in zip(routed[1:], rounds[1:])
        ]

    stages = (send_in, work, send_rows, send_columns)
    held, finished = {}, {}
    out = None
    for tick in range(begins[-1] + len(stages)):
        now = {}
        for slot, begin in enumerate(begins):
            stage = tick - begin
            if stage == 0:
                now[slot] = send_in(slot)
            elif 0 < stage < len(stages):
                now[slot] = stages[stage](slot, held[slot])
            if stage == len(stages) - 1:
                finished[slot] = now.pop(slot)
                now[slot] = finished[slot][-1:]
        for first, count in gathers:
            if begins[first + count - 1] + len(stages) - 1 == tick:
                back = [piece for slot in range(first, first + count) for piece in finished[slot]]
                gathered = lax.all_gather(jnp.concatenate(back, axis=0), "dp", axis=0, tiled=True)
                out = unpack(ranks, inner, (first, count), per, place, gathered, out)
        wanted = [group_of[begins.index(tick + 1)]] if tick + 1 in begins else []
        now, ahead = lax.optimization_barrier((now, [ready[g] for g in wanted]))
        for g, value in zip(wanted, ahead):
            ready[g] = value
        held.update(now)
    return out.reshape(grads.shape)


def solution(mesh):
    placed = (
        P("dp", None, None, "fsdp"),
        P("fsdp", "dp", None, None),
        P("fsdp", "dp", None, None),
        P("fsdp", "dp", None, None),
        P("fsdp", "dp", None, None),
    )
    run = functools.partial(shards, mesh.shape["dp"], mesh.shape["fsdp"])
    return jax.shard_map(
        run, mesh=mesh, in_specs=placed, out_specs=P(None, None, "fsdp"), check_vma=False
    )
```

```python
import functools

import jax
import jax.numpy as jnp
from jax import lax
from jax.experimental import pallas as pl
from jax.experimental.pallas import tpu as pltpu
from jax.sharding import PartitionSpec as P

ema_decay = 0.999
MESH_AXES = ("dp", "fsdp")
VMEM_LIMIT = 60 * 1024 * 1024


def split(x):
    high = x.astype(jnp.bfloat16)
    low = (x - high.astype(jnp.float32)).astype(jnp.bfloat16)
    return high, low


def mm(a, b):
    return jnp.dot(a, b, preferred_element_type=jnp.float32)


def dot3(a, b):
    a_high, a_low = split(a)
    b_high, b_low = split(b)
    return mm(
        jnp.concatenate([a_high, a_high, a_low], axis=1), jnp.concatenate([b_high, b_low, b_high], axis=0)
    )


def fourth_kernel(left_ref, right_ref, left_out, right_out):
    for ref, out in ((left_ref, left_out), (right_ref, right_out)):
        root = ref[0, 0]
        square = dot3(root, root)
        out[0, 0] = dot3(square, square)


def fourth_powers(left_root, right_root):
    slabs, col_blocks, order, _ = left_root.shape
    spec = pl.BlockSpec((1, 1, order, order), lambda i, j: (i, j, 0, 0))
    shape = jax.ShapeDtypeStruct(left_root.shape, jnp.float32)
    count = slabs * col_blocks
    return pl.pallas_call(
        fourth_kernel,
        grid=(slabs, col_blocks),
        in_specs=[spec, spec],
        out_specs=[spec, spec],
        out_shape=[shape, shape],
        compiler_params=pltpu.CompilerParams(vmem_limit_bytes=VMEM_LIMIT),
        cost_estimate=pl.CostEstimate(
            flops=count * 4 * 3 * 2 * order**3, bytes_accessed=count * 16 * order**2, transcendentals=0
        ),
        name="fourth_powers",
    )(left_root, right_root)


def slab_of(k, e, outer_place, inner_place, inner):
    return (outer_place ^ k) * inner + (inner_place ^ e)


def pack_kernel(ranks, inner, place_ref, grads_ref, out_ref):
    d = pl.program_id(0)
    for k in range(ranks):
        for e in range(inner):
            slab = slab_of(k, e, d ^ place_ref[0], place_ref[1], inner)
            out_ref[0, e, 0, k] = grads_ref[slab, 0]


def pack(ranks, inner, slots, per, place, grads):
    first, count = slots
    slabs, order, width = grads.shape
    owners, rows = slabs // per, order // ranks
    packed = pl.pallas_call(
        functools.partial(pack_kernel, ranks, inner),
        grid=(ranks, count),
        in_specs=[
            pl.BlockSpec(memory_space=pltpu.SMEM),
            pl.BlockSpec((owners, 1, rows, width), lambda d, s: (0, first + s, d, 0)),
        ],
        out_specs=pl.BlockSpec((1, inner, 1, ranks, rows, width), lambda d, s: (d, 0, s, 0, 0, 0)),
        out_shape=jax.ShapeDtypeStruct((ranks, inner, count, ranks, rows, width), grads.dtype),
        compiler_params=pltpu.CompilerParams(vmem_limit_bytes=VMEM_LIMIT),
        cost_estimate=pl.CostEstimate(
            flops=0, bytes_accessed=4 * owners * count * order * width, transcendentals=0
        ),
        name="pack_slabs",
    )(place, grads.reshape(owners, per, order, width))
    return packed.reshape(-1, width)


def unpack_kernel(ranks, inner, place_ref, got_ref, *rest):
    out_ref = rest[-1]
    for k in range(ranks):
        for e in range(inner):
            slab = slab_of(k, e, place_ref[0], place_ref[1], inner)
            out_ref[slab, 0] = got_ref[0, 0, k * inner + e]


def unpack(ranks, inner, slots, per, place, got, so_far):
    first, count = slots
    width, owners = got.shape[1], ranks * inner
    rows = got.shape[0] // (ranks * owners * count)
    operands = [place, got.reshape(ranks, count, owners, rows, width)]
    operands += [] if so_far is None else [so_far]
    return pl.pallas_call(
        functools.partial(unpack_kernel, ranks, inner),
        grid=(ranks, count),
        in_specs=[
            pl.BlockSpec(memory_space=pltpu.SMEM),
            pl.BlockSpec((1, 1, owners, rows, width), lambda d, s: (d, s, 0, 0, 0)),
        ]
        + [pl.BlockSpec(memory_space=pl.ANY)] * (len(operands) - 2),
        out_specs=pl.BlockSpec((owners, 1, rows, width), lambda d, s: (0, first + s, d, 0)),
        out_shape=jax.ShapeDtypeStruct((owners, per, ranks * rows, width), got.dtype),
        input_output_aliases={} if so_far is None else {2: 0},
        compiler_params=pltpu.CompilerParams(vmem_limit_bytes=VMEM_LIMIT),
        cost_estimate=pl.CostEstimate(flops=0, bytes_accessed=4 * got.size, transcendentals=0),
        name="unpack_slabs",
    )(*operands)


def route_kernel(ranks, inner, place_ref, *refs):
    taken, outs, held = refs[:ranks], refs[ranks:-1], refs[-1]
    rows = outs[0].shape[0]
    turn, inner_place = place_ref[2] ^ place_ref[0], place_ref[1]
    for k in range(ranks):
        held[k] = taken[k][...]
    for m in range(ranks):
        for e in range(inner):
            start = pl.multiple_of((inner_place ^ e) * rows, rows)
            outs[m * inner + e][...] = held[turn ^ m, pl.ds(start, rows), :]


def route(ranks, inner, place, taken):
    rows, width = taken[0].shape[0] // inner, taken[0].shape[1]
    vmem = pl.BlockSpec(memory_space=pltpu.VMEM)
    return pl.pallas_call(
        functools.partial(route_kernel, ranks, inner),
        in_specs=[pl.BlockSpec(memory_space=pltpu.SMEM)] + [vmem] * ranks,
        out_specs=[vmem] * (ranks * inner),
        out_shape=[jax.ShapeDtypeStruct((rows, width), taken[0].dtype)] * (ranks * inner),
        scratch_shapes=[pltpu.VMEM((ranks, inner * rows, width), taken[0].dtype)],
        compiler_params=pltpu.CompilerParams(vmem_limit_bytes=VMEM_LIMIT // 4),
        cost_estimate=pl.CostEstimate(
            flops=0, bytes_accessed=4 * ranks * taken[0].size, transcendentals=0
        ),
        name="route",
    )(place, *taken)


def refine(root, fourth, stats):
    order = root.shape[0]
    coupled = dot3(fourth, stats)
    on_diagonal = lax.broadcasted_iota(jnp.int32, (order, order), 0) == lax.broadcasted_iota(
        jnp.int32, (order, order), 1
    )
    factor = (jnp.where(on_diagonal, 5.0, 0.0) - coupled) * 0.25
    return dot3(root, factor)


def block_kernel(ranks, inner, steps, place_ref, *refs):
    pieces = refs[:ranks]
    left_stats, right_stats, left_root, right_root, left_fourth, right_fourth = refs[ranks : ranks + 6]
    outs = refs[ranks + 6 : 2 * ranks + 6]
    blocks, results = refs[2 * ranks + 6 :]
    rows, width = pieces[0].shape[0] // inner, pieces[0].shape[1]
    order = blocks.shape[1]
    outer_place, inner_place = place_ref[0], place_ref[1]
    step = pl.program_id(0)
    per_block = order // width

    def spot(rank, shard):
        row = pl.multiple_of(rank * rows, rows)
        column = pl.multiple_of((shard % per_block) * width, width)
        return shard // per_block, pl.ds(row, rows), pl.ds(column, width)

    @pl.when(step == 0)
    def _():
        for k in range(ranks):
            for e in range(inner):
                blocks[spot(place_ref[2] ^ outer_place ^ k, inner_place ^ e)] = pieces[k][e * rows : (e + 1) * rows]

    block = blocks[step]
    turned = block.T
    left = ema_decay * left_stats[0, 0] + (1.0 - ema_decay) * mm(block, turned)
    right = ema_decay * right_stats[0, 0] + (1.0 - ema_decay) * mm(turned, block)
    new_left = refine(left_root[0, 0], left_fourth[0, 0], left)
    new_right = refine(right_root[0, 0], right_fourth[0, 0], right)
    halfway = mm(new_left.astype(jnp.bfloat16), block)
    results[step] = mm(halfway.astype(jnp.bfloat16), new_right.astype(jnp.bfloat16)).astype(results.dtype)

    @pl.when(step == steps - 1)
    def _():
        for k in range(ranks):
            for b in range(inner):
                outs[k][b * rows : (b + 1) * rows] = results[spot(place_ref[2] ^ k, b)]


def precondition(ranks, inner, slot, place, pieces, stats_and_roots):
    _, col_blocks, order, _ = stats_and_roots[0].shape
    strip = pl.BlockSpec(pieces[0].shape, lambda j: (0, 0))
    matrix = pl.BlockSpec((1, 1, order, order), lambda j: (slot, j, 0, 0))
    return pl.pallas_call(
        functools.partial(block_kernel, ranks, inner, col_blocks),
        grid=(col_blocks,),
        in_specs=[pl.BlockSpec(memory_space=pltpu.SMEM)] + [strip] * ranks + [matrix] * 6,
        out_specs=[strip] * ranks,
        out_shape=[jax.ShapeDtypeStruct(pieces[0].shape, jnp.bfloat16)] * ranks,
        scratch_shapes=[pltpu.VMEM((col_blocks, order, order), jnp.bfloat16)] * 2,
        compiler_params=pltpu.CompilerParams(vmem_limit_bytes=VMEM_LIMIT * 9 // 10),
        cost_estimate=pl.CostEstimate(
            flops=col_blocks * 16 * 2 * order**3,
            bytes_accessed=col_blocks * 28 * order**2,
            transcendentals=0,
        ),
        name="precondition",
    )(place, *pieces, *stats_and_roots)


def shards(ranks, fsdp, grads, left_stats, right_stats, left_root, right_root):
    per = left_stats.shape[0]
    inner = fsdp // ranks
    grads = grads[0]
    slabs, order, width = grads.shape
    rows = order // ranks
    f = lax.axis_index("fsdp")
    place = jnp.stack([f // inner, f % inner, lax.axis_index("dp")]).astype(jnp.int32)
    rounds = [(k, e) for k in range(ranks) for e in range(inner)]

    def number(d, a, b):
        return (d * ranks + a) * inner + b

    sources = [(d, a, b) for d in range(ranks) for a in range(ranks) for b in range(inner)]
    to_core = [
        [(a * inner + b, a * inner + (b ^ e)) for a in range(ranks) for b in range(inner)] for e in range(inner)
    ]
    to_owner = [
        [(number(d, a, b), number(a, d ^ a ^ k, b)) for d, a, b in sources] for k in range(ranks)
    ]
    to_row = [[(d, d ^ k) for d in range(ranks)] for k in range(ranks)]
    to_column = {
        (m, e): [(a * inner + b, (a ^ m) * inner + (b ^ e)) for a in range(ranks) for b in range(inner)]
        for m, e in rounds
    }

    half = max(per // 2, 1)
    sums = gathers = [(first, min(half, per - first)) for first in range(0, per, half)]
    begins = [slot + 2 * (slot // half) for slot in range(per)]
    group_of = [slot // half for slot in range(per)]
    ready = []
    for slots in sums:
        packed = pack(ranks, inner, slots, per, place, grads)
        ready.append([lax.psum_scatter(packed, "dp", scatter_dimension=0, tiled=True)])
    left_fourth, right_fourth = fourth_powers(left_root, right_root)
    ready[0], left_fourth, right_fourth = lax.optimization_barrier((ready[0], left_fourth, right_fourth))
    matrices = (left_stats, right_stats, left_root, right_root, left_fourth, right_fourth)

    def between_cores(g):
        parts = ready[g][0].reshape(inner, -1, width)
        ready[g] = [parts[0]] + [lax.ppermute(parts[e], "fsdp", to_core[e]) for e in range(1, inner)]

    def send_in(slot):
        g = group_of[slot]
        if slot == sums[g][0]:
            between_cores(g)
        at = (slot - sums[g][0]) * ranks
        strips = [
            jnp.concatenate([part[(at + k) * rows : (at + k + 1) * rows] for part in ready[g]], axis=0)
            for k in range(ranks)
        ]
        return [lax.ppermute(strips[k], MESH_AXES, to_owner[k]) for k in range(ranks)]

    def work(slot, arrived):
        return precondition(ranks, inner, slot, place, arrived, matrices)

    def send_rows(slot, strips):
        return [strips[0]] + [lax.ppermute(strips[k], "dp", to_row[k]) for k in range(1, ranks)]

    def send_columns(slot, moved):
        routed = route(ranks, inner, place, moved)
        return [routed[0]] + [
            lax.ppermute(piece, "fsdp", to_column[key]) for piece, key in zip(routed[1:], rounds[1:])
        ]

    stages = (send_in, work, send_rows, send_columns)
    held, finished = {}, {}
    out = None
    for tick in range(begins[-1] + len(stages)):
        now = {}
        for slot, begin in enumerate(begins):
            stage = tick - begin
            if stage == 0:
                now[slot] = send_in(slot)
            elif 0 < stage < len(stages):
                now[slot] = stages[stage](slot, held[slot])
            if stage == len(stages) - 1:
                finished[slot] = now.pop(slot)
                now[slot] = finished[slot][-1:]
        for first, count in gathers:
            if begins[first + count - 1] + len(stages) - 1 == tick:
                back = [piece for slot in range(first, first + count) for piece in finished[slot]]
                gathered = lax.all_gather(jnp.concatenate(back, axis=0), "dp", axis=0, tiled=True)
                out = unpack(ranks, inner, (first, count), per, place, gathered, out)
        wanted = [group_of[begins.index(tick + 1)]] if tick + 1 in begins else []
        now, ahead = lax.optimization_barrier((now, [ready[g] for g in wanted]))
        for g, value in zip(wanted, ahead):
            ready[g] = value
        held.update(now)
    return out.reshape(grads.shape)


def solution(mesh):
    placed = (
        P("dp", None, None, "fsdp"),
        P("fsdp", "dp", None, None),
        P("fsdp", "dp", None, None),
        P("fsdp", "dp", None, None),
        P("fsdp", "dp", None, None),
    )
    run = functools.partial(shards, mesh.shape["dp"], mesh.shape["fsdp"])
    return jax.shard_map(
        run, mesh=mesh, in_specs=placed, out_specs=P(None, None, "fsdp"), check_vma=False
    )
```

```python
import functools

import jax
import jax.numpy as jnp
from jax import lax
from jax.experimental import pallas as pl
from jax.experimental.pallas import tpu as pltpu
from jax.sharding import PartitionSpec as P

ema_decay = 0.999
MESH_AXES = ("dp", "fsdp")
VMEM_LIMIT = 60 * 1024 * 1024


def split(x):
    high = x.astype(jnp.bfloat16)
    low = (x - high.astype(jnp.float32)).astype(jnp.bfloat16)
    return high, low


def mm(a, b):
    return jnp.dot(a, b, preferred_element_type=jnp.float32)


def dot3(a, b):
    a_high, a_low = split(a)
    b_high, b_low = split(b)
    return mm(
        jnp.concatenate([a_high, a_high, a_low], axis=1), jnp.concatenate([b_high, b_low, b_high], axis=0)
    )


def fourth_kernel(left_ref, right_ref, left_out, right_out):
    for ref, out in ((left_ref, left_out), (right_ref, right_out)):
        root = ref[0, 0]
        square = dot3(root, root)
        out[0, 0] = dot3(square, square)


def fourth_powers(left_root, right_root):
    slabs, col_blocks, order, _ = left_root.shape
    spec = pl.BlockSpec((1, 1, order, order), lambda i, j: (i, j, 0, 0))
    shape = jax.ShapeDtypeStruct(left_root.shape, jnp.float32)
    count = slabs * col_blocks
    return pl.pallas_call(
        fourth_kernel,
        grid=(slabs, col_blocks),
        in_specs=[spec, spec],
        out_specs=[spec, spec],
        out_shape=[shape, shape],
        compiler_params=pltpu.CompilerParams(vmem_limit_bytes=VMEM_LIMIT),
        cost_estimate=pl.CostEstimate(
            flops=count * 4 * 3 * 2 * order**3, bytes_accessed=count * 16 * order**2, transcendentals=0
        ),
        name="fourth_powers",
    )(left_root, right_root)


def slab_of(k, e, outer_place, inner_place, inner):
    return (outer_place ^ k) * inner + (inner_place ^ e)


def pack_kernel(ranks, inner, place_ref, grads_ref, out_ref):
    d = pl.program_id(0)
    for k in range(ranks):
        for e in range(inner):
            slab = slab_of(k, e, d ^ place_ref[0], place_ref[1], inner)
            out_ref[0, e, 0, k] = grads_ref[slab, 0]


def pack(ranks, inner, slots, per, place, grads):
    first, count = slots
    slabs, order, width = grads.shape
    owners, rows = slabs // per, order // ranks
    packed = pl.pallas_call(
        functools.partial(pack_kernel, ranks, inner),
        grid=(ranks, count),
        in_specs=[
            pl.BlockSpec(memory_space=pltpu.SMEM),
            pl.BlockSpec((owners, 1, rows, width), lambda d, s: (0, first + s, d, 0)),
        ],
        out_specs=pl.BlockSpec((1, inner, 1, ranks, rows, width), lambda d, s: (d, 0, s, 0, 0, 0)),
        out_shape=jax.ShapeDtypeStruct((ranks, inner, count, ranks, rows, width), grads.dtype),
        compiler_params=pltpu.CompilerParams(vmem_limit_bytes=VMEM_LIMIT),
        cost_estimate=pl.CostEstimate(
            flops=0, bytes_accessed=4 * owners * count * order * width, transcendentals=0
        ),
        name="pack_slabs",
    )(place, grads.reshape(owners, per, order, width))
    return packed.reshape(-1, width)


def unpack_kernel(ranks, inner, place_ref, got_ref, *rest):
    out_ref = rest[-1]
    for k in range(ranks):
        for e in range(inner):
            slab = slab_of(k, e, place_ref[0], place_ref[1], inner)
            out_ref[slab, 0] = got_ref[0, 0, k * inner + e]


def unpack(ranks, inner, slots, per, place, got, so_far):
    first, count = slots
    width, owners = got.shape[1], ranks * inner
    rows = got.shape[0] // (ranks * owners * count)
    operands = [place, got.reshape(ranks, count, owners, rows, width)]
    operands += [] if so_far is None else [so_far]
    return pl.pallas_call(
        functools.partial(unpack_kernel, ranks, inner),
        grid=(ranks, count),
        in_specs=[
            pl.BlockSpec(memory_space=pltpu.SMEM),
            pl.BlockSpec((1, 1, owners, rows, width), lambda d, s: (d, s, 0, 0, 0)),
        ]
        + [pl.BlockSpec(memory_space=pl.ANY)] * (len(operands) - 2),
        out_specs=pl.BlockSpec((owners, 1, rows, width), lambda d, s: (0, first + s, d, 0)),
        out_shape=jax.ShapeDtypeStruct((owners, per, ranks * rows, width), got.dtype),
        input_output_aliases={} if so_far is None else {2: 0},
        compiler_params=pltpu.CompilerParams(vmem_limit_bytes=VMEM_LIMIT),
        cost_estimate=pl.CostEstimate(flops=0, bytes_accessed=4 * got.size, transcendentals=0),
        name="unpack_slabs",
    )(*operands)


def route_kernel(ranks, inner, place_ref, *refs):
    taken, outs, held = refs[:ranks], refs[ranks:-1], refs[-1]
    rows = outs[0].shape[0]
    turn, inner_place = place_ref[2] ^ place_ref[0], place_ref[1]
    for k in range(ranks):
        held[k] = taken[k][...]
    for m in range(ranks):
        for e in range(inner):
            start = pl.multiple_of((inner_place ^ e) * rows, rows)
            outs[m * inner + e][...] = held[turn ^ m, pl.ds(start, rows), :]


def route(ranks, inner, place, taken):
    rows, width = taken[0].shape[0] // inner, taken[0].shape[1]
    vmem = pl.BlockSpec(memory_space=pltpu.VMEM)
    return pl.pallas_call(
        functools.partial(route_kernel, ranks, inner),
        in_specs=[pl.BlockSpec(memory_space=pltpu.SMEM)] + [vmem] * ranks,
        out_specs=[vmem] * (ranks * inner),
        out_shape=[jax.ShapeDtypeStruct((rows, width), taken[0].dtype)] * (ranks * inner),
        scratch_shapes=[pltpu.VMEM((ranks, inner * rows, width), taken[0].dtype)],
        compiler_params=pltpu.CompilerParams(vmem_limit_bytes=VMEM_LIMIT // 4),
        cost_estimate=pl.CostEstimate(
            flops=0, bytes_accessed=4 * ranks * taken[0].size, transcendentals=0
        ),
        name="route",
    )(place, *taken)


def refine(root, fourth, stats):
    order = root.shape[0]
    coupled = dot3(fourth, stats)
    on_diagonal = lax.broadcasted_iota(jnp.int32, (order, order), 0) == lax.broadcasted_iota(
        jnp.int32, (order, order), 1
    )
    factor = (jnp.where(on_diagonal, 5.0, 0.0) - coupled) * 0.25
    return dot3(root, factor)


def block_kernel(ranks, inner, steps, place_ref, *refs):
    pieces = refs[:ranks]
    left_stats, right_stats, left_root, right_root, left_fourth, right_fourth = refs[ranks : ranks + 6]
    outs = refs[ranks + 6 : 2 * ranks + 6]
    blocks, results = refs[2 * ranks + 6 :]
    rows, width = pieces[0].shape[0] // inner, pieces[0].shape[1]
    order = blocks.shape[1]
    outer_place, inner_place = place_ref[0], place_ref[1]
    step = pl.program_id(0)
    per_block = order // width

    def spot(rank, shard):
        row = pl.multiple_of(rank * rows, rows)
        column = pl.multiple_of((shard % per_block) * width, width)
        return shard // per_block, pl.ds(row, rows), pl.ds(column, width)

    @pl.when(step == 0)
    def _():
        for k in range(ranks):
            for e in range(inner):
                blocks[spot(place_ref[2] ^ outer_place ^ k, inner_place ^ e)] = pieces[k][e * rows : (e + 1) * rows]

    block = blocks[step]
    turned = block.T
    left = ema_decay * left_stats[0, 0] + (1.0 - ema_decay) * mm(block, turned)
    right = ema_decay * right_stats[0, 0] + (1.0 - ema_decay) * mm(turned, block)
    new_left = refine(left_root[0, 0], left_fourth[0, 0], left)
    new_right = refine(right_root[0, 0], right_fourth[0, 0], right)
    halfway = mm(new_left.astype(jnp.bfloat16), block)
    results[step] = mm(halfway.astype(jnp.bfloat16), new_right.astype(jnp.bfloat16)).astype(results.dtype)

    @pl.when(step == steps - 1)
    def _():
        for k in range(ranks):
            for b in range(inner):
                outs[k][b * rows : (b + 1) * rows] = results[spot(place_ref[2] ^ k, b)]


def precondition(ranks, inner, slot, place, pieces, stats_and_roots):
    _, col_blocks, order, _ = stats_and_roots[0].shape
    strip = pl.BlockSpec(pieces[0].shape, lambda j: (0, 0))
    matrix = pl.BlockSpec((1, 1, order, order), lambda j: (slot, j, 0, 0))
    return pl.pallas_call(
        functools.partial(block_kernel, ranks, inner, col_blocks),
        grid=(col_blocks,),
        in_specs=[pl.BlockSpec(memory_space=pltpu.SMEM)] + [strip] * ranks + [matrix] * 6,
        out_specs=[strip] * ranks,
        out_shape=[jax.ShapeDtypeStruct(pieces[0].shape, jnp.bfloat16)] * ranks,
        scratch_shapes=[pltpu.VMEM((col_blocks, order, order), jnp.bfloat16)] * 2,
        compiler_params=pltpu.CompilerParams(vmem_limit_bytes=VMEM_LIMIT * 9 // 10),
        cost_estimate=pl.CostEstimate(
            flops=col_blocks * 16 * 2 * order**3,
            bytes_accessed=col_blocks * 28 * order**2,
            transcendentals=0,
        ),
        name="precondition",
    )(place, *pieces, *stats_and_roots)


def shards(ranks, fsdp, grads, left_stats, right_stats, left_root, right_root):
    per = left_stats.shape[0]
    inner = fsdp // ranks
    grads = grads[0]
    slabs, order, width = grads.shape
    rows = order // ranks
    f = lax.axis_index("fsdp")
    place = jnp.stack([f // inner, f % inner, lax.axis_index("dp")]).astype(jnp.int32)
    rounds = [(k, e) for k in range(ranks) for e in range(inner)]

    def number(d, a, b):
        return (d * ranks + a) * inner + b

    sources = [(d, a, b) for d in range(ranks) for a in range(ranks) for b in range(inner)]
    to_core = [
        [(a * inner + b, a * inner + (b ^ e)) for a in range(ranks) for b in range(inner)] for e in range(inner)
    ]
    to_owner = [
        [(number(d, a, b), number(a, d ^ a ^ k, b)) for d, a, b in sources] for k in range(ranks)
    ]
    to_row = [[(d, d ^ k) for d in range(ranks)] for k in range(ranks)]
    to_column = {
        (m, e): [(a * inner + b, (a ^ m) * inner + (b ^ e)) for a in range(ranks) for b in range(inner)]
        for m, e in rounds
    }

    half = max(per // 2, 1)
    sums = gathers = [(first, min(half, per - first)) for first in range(0, per, half)]
    begins = [slot + 2 * (slot // half) for slot in range(per)]
    group_of = [slot // half for slot in range(per)]
    ready = []
    for slots in sums:
        packed = pack(ranks, inner, slots, per, place, grads)
        ready.append([lax.psum_scatter(packed, "dp", scatter_dimension=0, tiled=True)])
    left_fourth, right_fourth = fourth_powers(left_root, right_root)
    ready[0], left_fourth, right_fourth = lax.optimization_barrier((ready[0], left_fourth, right_fourth))
    matrices = (left_stats, right_stats, left_root, right_root, left_fourth, right_fourth)

    def between_cores(g):
        parts = ready[g][0].reshape(inner, -1, width)
        ready[g] = [parts[0]] + [lax.ppermute(parts[e], "fsdp", to_core[e]) for e in range(1, inner)]

    def send_in(slot):
        g = group_of[slot]
        if slot == sums[g][0]:
            between_cores(g)
        at = (slot - sums[g][0]) * ranks
        strips = [
            jnp.concatenate([part[(at + k) * rows : (at + k + 1) * rows] for part in ready[g]], axis=0)
            for k in range(ranks)
        ]
        return [lax.ppermute(strips[k], MESH_AXES, to_owner[k]) for k in range(ranks)]

    def work(slot, arrived):
        return precondition(ranks, inner, slot, place, arrived, matrices)

    def send_rows(slot, strips):
        return [strips[0]] + [lax.ppermute(strips[k], "dp", to_row[k]) for k in range(1, ranks)]

    def send_columns(slot, moved):
        routed = route(ranks, inner, place, moved)
        back = [routed[0]] + [
            lax.ppermute(piece, "fsdp", to_column[key]) for piece, key in zip(routed[1:], rounds[1:])
        ]
        g = group_of[slot] + 1
        if slot + 1 < per and group_of[slot + 1] == g:
            at = len(back) // 2
            back[at], ready[g][0] = lax.optimization_barrier((back[at], ready[g][0]))
        return back

    stages = (send_in, work, send_rows, send_columns)
    held, finished = {}, {}
    out = None
    for tick in range(begins[-1] + len(stages)):
        now = {}
        for slot, begin in enumerate(begins):
            stage = tick - begin
            if stage == 0:
                now[slot] = send_in(slot)
            elif 0 < stage < len(stages):
                now[slot] = stages[stage](slot, held[slot])
            if stage == len(stages) - 1:
                finished[slot] = now.pop(slot)
                now[slot] = finished[slot][-1:]
        for first, count in gathers:
            if begins[first + count - 1] + len(stages) - 1 == tick:
                back = [piece for slot in range(first, first + count) for piece in finished[slot]]
                gathered = lax.all_gather(jnp.concatenate(back, axis=0), "dp", axis=0, tiled=True)
                out = unpack(ranks, inner, (first, count), per, place, gathered, out)
        after = begins.index(tick + 1) if tick + 1 in begins else None
        wanted = [] if after is None or after % half == 0 else [group_of[after]]
        now, ahead = lax.optimization_barrier((now, [ready[g] for g in wanted]))
        for g, value in zip(wanted, ahead):
            ready[g] = value
        held.update(now)
    return out.reshape(grads.shape)


def solution(mesh):
    placed = (
        P("dp", None, None, "fsdp"),
        P("fsdp", "dp", None, None),
        P("fsdp", "dp", None, None),
        P("fsdp", "dp", None, None),
        P("fsdp", "dp", None, None),
    )
    run = functools.partial(shards, mesh.shape["dp"], mesh.shape["fsdp"])
    return jax.shard_map(
        run, mesh=mesh, in_specs=placed, out_specs=P(None, None, "fsdp"), check_vma=False
    )
```

```python
import functools

import jax
import jax.numpy as jnp
from jax import lax
from jax.experimental import pallas as pl
from jax.experimental.pallas import tpu as pltpu
from jax.sharding import PartitionSpec as P

ema_decay = 0.999
MESH_AXES = ("dp", "fsdp")
VMEM_LIMIT = 60 * 1024 * 1024


def split(x):
    high = x.astype(jnp.bfloat16)
    low = (x - high.astype(jnp.float32)).astype(jnp.bfloat16)
    return high, low


def mm(a, b):
    return jnp.dot(a, b, preferred_element_type=jnp.float32)


def dot3(a, b):
    a_high, a_low = split(a)
    b_high, b_low = split(b)
    return mm(
        jnp.concatenate([a_high, a_high, a_low], axis=1), jnp.concatenate([b_high, b_low, b_high], axis=0)
    )


def fourth_kernel(left_ref, right_ref, left_out, right_out):
    for ref, out in ((left_ref, left_out), (right_ref, right_out)):
        root = ref[0, 0]
        square = dot3(root, root)
        out[0, 0] = dot3(square, square)


def fourth_powers(left_root, right_root):
    slabs, col_blocks, order, _ = left_root.shape
    spec = pl.BlockSpec((1, 1, order, order), lambda i, j: (i, j, 0, 0))
    shape = jax.ShapeDtypeStruct(left_root.shape, jnp.float32)
    count = slabs * col_blocks
    return pl.pallas_call(
        fourth_kernel,
        grid=(slabs, col_blocks),
        in_specs=[spec, spec],
        out_specs=[spec, spec],
        out_shape=[shape, shape],
        compiler_params=pltpu.CompilerParams(vmem_limit_bytes=VMEM_LIMIT),
        cost_estimate=pl.CostEstimate(
            flops=count * 4 * 3 * 2 * order**3, bytes_accessed=count * 16 * order**2, transcendentals=0
        ),
        name="fourth_powers",
    )(left_root, right_root)


def slab_of(k, e, outer_place, inner_place, inner):
    return (outer_place ^ k) * inner + (inner_place ^ e)


def pack_kernel(ranks, inner, place_ref, grads_ref, out_ref):
    d = pl.program_id(0)
    for k in range(ranks):
        for e in range(inner):
            slab = slab_of(k, e, d ^ place_ref[0], place_ref[1], inner)
            out_ref[0, e, 0, k] = grads_ref[slab, 0]


def pack(ranks, inner, slots, per, place, grads):
    first, count = slots
    slabs, order, width = grads.shape
    owners, rows = slabs // per, order // ranks
    packed = pl.pallas_call(
        functools.partial(pack_kernel, ranks, inner),
        grid=(ranks, count),
        in_specs=[
            pl.BlockSpec(memory_space=pltpu.SMEM),
            pl.BlockSpec((owners, 1, rows, width), lambda d, s: (0, first + s, d, 0)),
        ],
        out_specs=pl.BlockSpec((1, inner, 1, ranks, rows, width), lambda d, s: (d, 0, s, 0, 0, 0)),
        out_shape=jax.ShapeDtypeStruct((ranks, inner, count, ranks, rows, width), grads.dtype),
        compiler_params=pltpu.CompilerParams(vmem_limit_bytes=VMEM_LIMIT),
        cost_estimate=pl.CostEstimate(
            flops=0, bytes_accessed=4 * owners * count * order * width, transcendentals=0
        ),
        name="pack_slabs",
    )(place, grads.reshape(owners, per, order, width))
    return packed.reshape(-1, width)


def unpack_kernel(ranks, inner, place_ref, got_ref, *rest):
    out_ref = rest[-1]
    for k in range(ranks):
        for e in range(inner):
            slab = slab_of(k, e, place_ref[0], place_ref[1], inner)
            out_ref[slab, 0] = got_ref[0, 0, k * inner + e]


def unpack(ranks, inner, slots, per, place, got, so_far):
    first, count = slots
    width, owners = got.shape[1], ranks * inner
    rows = got.shape[0] // (ranks * owners * count)
    operands = [place, got.reshape(ranks, count, owners, rows, width)]
    operands += [] if so_far is None else [so_far]
    return pl.pallas_call(
        functools.partial(unpack_kernel, ranks, inner),
        grid=(ranks, count),
        in_specs=[
            pl.BlockSpec(memory_space=pltpu.SMEM),
            pl.BlockSpec((1, 1, owners, rows, width), lambda d, s: (d, s, 0, 0, 0)),
        ]
        + [pl.BlockSpec(memory_space=pl.ANY)] * (len(operands) - 2),
        out_specs=pl.BlockSpec((owners, 1, rows, width), lambda d, s: (0, first + s, d, 0)),
        out_shape=jax.ShapeDtypeStruct((owners, per, ranks * rows, width), got.dtype),
        input_output_aliases={} if so_far is None else {2: 0},
        compiler_params=pltpu.CompilerParams(vmem_limit_bytes=VMEM_LIMIT),
        cost_estimate=pl.CostEstimate(flops=0, bytes_accessed=4 * got.size, transcendentals=0),
        name="unpack_slabs",
    )(*operands)


def route_kernel(ranks, inner, place_ref, *refs):
    taken, outs, held = refs[:ranks], refs[ranks:-1], refs[-1]
    rows = outs[0].shape[0]
    turn, inner_place = place_ref[2] ^ place_ref[0], place_ref[1]
    for k in range(ranks):
        held[k] = taken[k][...]
    for m in range(ranks):
        for e in range(inner):
            start = pl.multiple_of((inner_place ^ e) * rows, rows)
            outs[m * inner + e][...] = held[turn ^ m, pl.ds(start, rows), :]


def route(ranks, inner, place, taken):
    rows, width = taken[0].shape[0] // inner, taken[0].shape[1]
    vmem = pl.BlockSpec(memory_space=pltpu.VMEM)
    return pl.pallas_call(
        functools.partial(route_kernel, ranks, inner),
        in_specs=[pl.BlockSpec(memory_space=pltpu.SMEM)] + [vmem] * ranks,
        out_specs=[vmem] * (ranks * inner),
        out_shape=[jax.ShapeDtypeStruct((rows, width), taken[0].dtype)] * (ranks * inner),
        scratch_shapes=[pltpu.VMEM((ranks, inner * rows, width), taken[0].dtype)],
        compiler_params=pltpu.CompilerParams(vmem_limit_bytes=VMEM_LIMIT // 4),
        cost_estimate=pl.CostEstimate(
            flops=0, bytes_accessed=4 * ranks * taken[0].size, transcendentals=0
        ),
        name="route",
    )(place, *taken)


def refine(root, fourth, stats):
    order = root.shape[0]
    coupled = dot3(fourth, stats)
    on_diagonal = lax.broadcasted_iota(jnp.int32, (order, order), 0) == lax.broadcasted_iota(
        jnp.int32, (order, order), 1
    )
    factor = (jnp.where(on_diagonal, 5.0, 0.0) - coupled) * 0.25
    return dot3(root, factor)


def block_kernel(ranks, inner, steps, place_ref, *refs):
    pieces = refs[:ranks]
    left_stats, right_stats, left_root, right_root, left_fourth, right_fourth = refs[ranks : ranks + 6]
    outs = refs[ranks + 6 : 2 * ranks + 6]
    blocks, results = refs[2 * ranks + 6 :]
    rows, width = pieces[0].shape[0] // inner, pieces[0].shape[1]
    order = blocks.shape[1]
    outer_place, inner_place = place_ref[0], place_ref[1]
    step = pl.program_id(0)
    per_block = order // width

    def spot(rank, shard):
        row = pl.multiple_of(rank * rows, rows)
        column = pl.multiple_of((shard % per_block) * width, width)
        return shard // per_block, pl.ds(row, rows), pl.ds(column, width)

    @pl.when(step == 0)
    def _():
        for k in range(ranks):
            for e in range(inner):
                blocks[spot(place_ref[2] ^ outer_place ^ k, inner_place ^ e)] = pieces[k][e * rows : (e + 1) * rows]

    block = blocks[step]
    turned = block.T
    left = ema_decay * left_stats[0, 0] + (1.0 - ema_decay) * mm(block, turned)
    right = ema_decay * right_stats[0, 0] + (1.0 - ema_decay) * mm(turned, block)
    new_left = refine(left_root[0, 0], left_fourth[0, 0], left)
    new_right = refine(right_root[0, 0], right_fourth[0, 0], right)
    halfway = mm(new_left.astype(jnp.bfloat16), block)
    results[step] = mm(halfway.astype(jnp.bfloat16), new_right.astype(jnp.bfloat16)).astype(results.dtype)

    @pl.when(step == steps - 1)
    def _():
        for k in range(ranks):
            for b in range(inner):
                outs[k][b * rows : (b + 1) * rows] = results[spot(place_ref[2] ^ k, b)]


def precondition(ranks, inner, slot, place, pieces, stats_and_roots):
    _, col_blocks, order, _ = stats_and_roots[0].shape
    strip = pl.BlockSpec(pieces[0].shape, lambda j: (0, 0))
    matrix = pl.BlockSpec((1, 1, order, order), lambda j: (slot, j, 0, 0))
    return pl.pallas_call(
        functools.partial(block_kernel, ranks, inner, col_blocks),
        grid=(col_blocks,),
        in_specs=[pl.BlockSpec(memory_space=pltpu.SMEM)] + [strip] * ranks + [matrix] * 6,
        out_specs=[strip] * ranks,
        out_shape=[jax.ShapeDtypeStruct(pieces[0].shape, jnp.bfloat16)] * ranks,
        scratch_shapes=[pltpu.VMEM((col_blocks, order, order), jnp.bfloat16)] * 2,
        compiler_params=pltpu.CompilerParams(vmem_limit_bytes=VMEM_LIMIT * 9 // 10),
        cost_estimate=pl.CostEstimate(
            flops=col_blocks * 16 * 2 * order**3,
            bytes_accessed=col_blocks * 28 * order**2,
            transcendentals=0,
        ),
        name="precondition",
    )(place, *pieces, *stats_and_roots)


def shards(ranks, fsdp, grads, left_stats, right_stats, left_root, right_root):
    per = left_stats.shape[0]
    inner = fsdp // ranks
    grads = grads[0]
    slabs, order, width = grads.shape
    rows = order // ranks
    f = lax.axis_index("fsdp")
    place = jnp.stack([f // inner, f % inner, lax.axis_index("dp")]).astype(jnp.int32)
    rounds = [(k, e) for k in range(ranks) for e in range(inner)]

    def number(d, a, b):
        return (d * ranks + a) * inner + b

    sources = [(d, a, b) for d in range(ranks) for a in range(ranks) for b in range(inner)]
    to_core = [
        [(a * inner + b, a * inner + (b ^ e)) for a in range(ranks) for b in range(inner)] for e in range(inner)
    ]
    to_owner = [
        [(number(d, a, b), number(a, d ^ a ^ k, b)) for d, a, b in sources] for k in range(ranks)
    ]
    to_row = [[(d, d ^ k) for d in range(ranks)] for k in range(ranks)]
    to_column = {
        (m, e): [(a * inner + b, (a ^ m) * inner + (b ^ e)) for a in range(ranks) for b in range(inner)]
        for m, e in rounds
    }

    half = max(per // 2, 1)
    sums = gathers = [(first, min(half, per - first)) for first in range(0, per, half)]
    begins = [slot + 2 * (slot // half) for slot in range(per)]
    group_of = [slot // half for slot in range(per)]
    ready = []
    for slots in sums:
        packed = pack(ranks, inner, slots, per, place, grads)
        ready.append([lax.psum_scatter(packed, "dp", scatter_dimension=0, tiled=True)])
    left_fourth, right_fourth = fourth_powers(left_root, right_root)
    ready[0], left_fourth, right_fourth = lax.optimization_barrier((ready[0], left_fourth, right_fourth))
    matrices = (left_stats, right_stats, left_root, right_root, left_fourth, right_fourth)

    def between_cores(g):
        parts = ready[g][0].reshape(inner, -1, width)
        ready[g] = [parts[0]] + [lax.ppermute(parts[e], "fsdp", to_core[e]) for e in range(1, inner)]

    def send_in(slot):
        g = group_of[slot]
        if slot == sums[g][0]:
            between_cores(g)
        at = (slot - sums[g][0]) * ranks
        strips = [
            jnp.concatenate([part[(at + k) * rows : (at + k + 1) * rows] for part in ready[g]], axis=0)
            for k in range(ranks)
        ]
        return [lax.ppermute(strips[k], MESH_AXES, to_owner[k]) for k in range(ranks)]

    def work(slot, arrived):
        return precondition(ranks, inner, slot, place, arrived, matrices)

    def send_rows(slot, strips):
        return [strips[0]] + [lax.ppermute(strips[k], "dp", to_row[k]) for k in range(1, ranks)]

    def send_columns(slot, moved, now):
        routed = list(route(ranks, inner, place, moved))
        if slot + 1 in now:
            middle = len(routed) // 2
            routed[middle:], now[slot + 1][-1] = lax.optimization_barrier((routed[middle:], now[slot + 1][-1]))
        back = [routed[0]] + [
            lax.ppermute(piece, "fsdp", to_column[key]) for piece, key in zip(routed[1:], rounds[1:])
        ]
        g = group_of[slot] + 1
        if slot + 1 < per and group_of[slot + 1] == g:
            at = len(back) // 2
            back[at], ready[g][0] = lax.optimization_barrier((back[at], ready[g][0]))
        return back

    stages = 4
    held, finished = {}, {}
    out = None
    for tick in range(begins[-1] + stages):
        now = {}
        at_stage = {tick - begin: slot for slot, begin in enumerate(begins)}
        for stage in (2, 3, 0, 1):
            if stage not in at_stage:
                continue
            slot = at_stage[stage]
            if stage == 0:
                now[slot] = send_in(slot)
            elif stage == 1:
                now[slot] = work(slot, held[slot])
            elif stage == 2:
                now[slot] = send_rows(slot, held[slot])
            else:
                finished[slot] = send_columns(slot, held[slot], now)
                now[slot] = finished[slot][-1:]
        for first, count in gathers:
            if begins[first + count - 1] + stages - 1 == tick:
                back = [piece for slot in range(first, first + count) for piece in finished[slot]]
                gathered = lax.all_gather(jnp.concatenate(back, axis=0), "dp", axis=0, tiled=True)
                out = unpack(ranks, inner, (first, count), per, place, gathered, out)
        after = begins.index(tick + 1) if tick + 1 in begins else None
        wanted = [] if after is None or after % half == 0 else [group_of[after]]
        now, ahead = lax.optimization_barrier((now, [ready[g] for g in wanted]))
        for g, value in zip(wanted, ahead):
            ready[g] = value
        held.update(now)
    return out.reshape(grads.shape)


def solution(mesh):
    placed = (
        P("dp", None, None, "fsdp"),
        P("fsdp", "dp", None, None),
        P("fsdp", "dp", None, None),
        P("fsdp", "dp", None, None),
        P("fsdp", "dp", None, None),
    )
    run = functools.partial(shards, mesh.shape["dp"], mesh.shape["fsdp"])
    return jax.shard_map(
        run, mesh=mesh, in_specs=placed, out_specs=P(None, None, "fsdp"), check_vma=False
    )
```
